256 devices in a mesh: gx: 8 (over x, core), gy: 8 (over y, z_hi), gz: 4 (over z_lo).
Axes of the slice: x: 4, y: 4, z: 8 (z_hi: 2, z_lo: 4; z = z_hi * 4 + z_lo), core: 2. Of those that a mesh axis runs over, the one named last changes fastest.
Arguments:
- patches: bfloat16 [320, 5120], P(('gy', 'gz'), 'gx'), may hold values from -6 to 6
- merge_inner: bfloat16 [5120, 5120], P('gx', ('gy', 'gz')), may hold values from -0.078125 to 0.078125
- merge_outer: bfloat16 [5120, 8192], P(('gy', 'gz'), 'gx'), may hold values from -0.078125 to 0.078125
- gate_weight: bfloat16 [8192, 28672], P('gx', ('gy', 'gz')), may hold values from -0.0625 to 0.0625
- up_weight: bfloat16 [8192, 28672], P('gx', ('gy', 'gz')), may hold values from -0.0625 to 0.0625
- down_weight: bfloat16 [28672, 8192], P(('gy', 'gz'), 'gx'), may hold values from -0.03125 to 0.03125
- out_grad: bfloat16 [320, 8192], P(('gy', 'gz'), 'gx'), may hold values from -1.5 to 1.5
Outputs:
- patch_grad: bfloat16 [320, 5120], P(None, 'gx')
- inner_grad: bfloat16 [5120, 5120], P('gx', ('gy', 'gz'))
- outer_grad: bfloat16 [5120, 8192], P(('gy', 'gz'), 'gx')
- gate_grad: bfloat16 [8192, 28672], P('gx', ('gy', 'gz'))
- up_grad: bfloat16 [8192, 28672], P('gx', ('gy', 'gz'))
- down_grad: bfloat16 [28672, 8192], P(('gy', 'gz'), 'gx')
The draws below stay inside these ranges and needn't reach their ends.
All inputs are finite; a program needn't handle non-finite values.
Results may differ from the reference program's by a relative error of at most 0.015.
Values may be sent and summed in bfloat16 or wider, within the bound.
A program may use at most 64 MiB of HBM per device.

```python
import jax
import jax.numpy as jnp
from jax import lax

D = 8192
C = 5120
FF = 28672
TOKENS = 320


def block_scale(rng, shape, split, least, largest):
    gain = 1.0
    for dim, shards_of in split:
        heights = jax.random.uniform(jax.random.fold_in(jax.random.fold_in(rng, 6), dim), (shards_of,), jnp.float32, least / len(split), largest / len(split))
        gain = gain * jnp.repeat(jnp.exp(heights), shape[dim] // shards_of).reshape((-1,) + (1,) * (len(shape) - 1 - dim))
    return gain


def normal_values(stream_key, dims, scale, reach, cuts=(), dtype=jnp.bfloat16):
    result = scale * jax.random.normal(stream_key, dims, jnp.float32)
    if cuts:
        result = result * block_scale(stream_key, dims, cuts, -0.22, 0.18)
    return jnp.clip(result, -reach, reach).astype(dtype)


def setup_inputs(seed: int = 0) -> dict:
    splits = jax.random.split(jax.random.key(seed), 8)
    patches = normal_values(splits[0], (TOKENS, C), 1.0, 6.0, ((0, 32), (1, 8)))
    merge_inner = normal_values(splits[1], (C, C), C ** -0.5, 0.078125, ((0, 8), (1, 32)))
    merge_outer = normal_values(splits[2], (C, D), C ** -0.5, 0.078125, ((0, 32), (1, 8)))
    gate_weight = normal_values(splits[3], (D, FF), D ** -0.5, 0.0625, ((0, 8), (1, 32)))
    up_weight = normal_values(splits[4], (D, FF), D ** -0.5, 0.0625, ((0, 8), (1, 32)))
    down_weight = normal_values(splits[5], (FF, D), FF ** -0.5, 0.03125, ((0, 32), (1, 8)))
    out_grad = normal_values(splits[6], (TOKENS, D), 0.25, 1.5, ((0, 32), (1, 8)))
    return {"patches": patches, "merge_inner": merge_inner, "merge_outer": merge_outer, "gate_weight": gate_weight, "up_weight": up_weight, "down_weight": down_weight, "out_grad": out_grad}


def gelu_parts(pre_act):
    normal_cdf = 0.5 * (1.0 + lax.erf(pre_act * 0.7071067811865476))
    normal_pdf = jnp.exp(-0.5 * pre_act * pre_act) * 0.3989422804014327
    return pre_act * normal_cdf, normal_cdf + pre_act * normal_pdf


def swiglu_backward(gate_sum, up_sum, down_sum):
    logistic = jax.nn.sigmoid(gate_sum)
    swish_value = gate_sum * logistic
    swish_slope = logistic * (1.0 + gate_sum * (1.0 - logistic))
    hidden = (swish_value * up_sum).astype(jnp.bfloat16)
    gate_in = (down_sum * up_sum * swish_slope).astype(jnp.bfloat16)
    up_in = (down_sum * swish_value).astype(jnp.bfloat16)
    return hidden, gate_in, up_in


def reference(patches, merge_inner, merge_outer, gate_weight, up_weight, down_weight, out_grad):
    pre_act = jnp.dot(patches, merge_inner, preferred_element_type=jnp.float32)
    gelu_value, gelu_slope = gelu_parts(pre_act)
    merger_hidden = gelu_value.astype(jnp.bfloat16)
    merged = jnp.dot(merger_hidden, merge_outer, preferred_element_type=jnp.float32).astype(jnp.bfloat16)
    gate_sum = jnp.dot(merged, gate_weight, preferred_element_type=jnp.float32)
    up_sum = jnp.dot(merged, up_weight, preferred_element_type=jnp.float32)
    down_sum = jnp.dot(out_grad, down_weight.T, preferred_element_type=jnp.float32)
    hidden, gate_in, up_in = swiglu_backward(gate_sum, up_sum, down_sum)
    down_grad = jnp.dot(hidden.T, out_grad, preferred_element_type=jnp.float32).astype(jnp.bfloat16)
    gate_grad = jnp.dot(merged.T, gate_in, preferred_element_type=jnp.float32).astype(jnp.bfloat16)
    up_grad = jnp.dot(merged.T, up_in, preferred_element_type=jnp.float32).astype(jnp.bfloat16)
    back_sum = jnp.dot(gate_in, gate_weight.T, preferred_element_type=jnp.float32)
    back_sum = back_sum + jnp.dot(up_in, up_weight.T, preferred_element_type=jnp.float32)
    merged_grad = (out_grad.astype(jnp.float32) + back_sum).astype(jnp.bfloat16)
    outer_grad = jnp.dot(merger_hidden.T, merged_grad, preferred_element_type=jnp.float32).astype(jnp.bfloat16)
    act_grad = jnp.dot(merged_grad, merge_outer.T, preferred_element_type=jnp.float32)
    pre_grad = (act_grad * gelu_slope).astype(jnp.bfloat16)
    inner_grad = jnp.dot(patches.T, pre_grad, preferred_element_type=jnp.float32).astype(jnp.bfloat16)
    patch_grad = jnp.dot(pre_grad, merge_inner.T, preferred_element_type=jnp.float32).astype(jnp.bfloat16)
    return patch_grad, inner_grad, outer_grad, gate_grad, up_grad, down_grad
```

```python
import jax
import jax.numpy as jnp
from jax import lax
from jax.experimental import pallas as pl
from jax.experimental.pallas import tpu as pltpu
from jax.sharding import PartitionSpec as P

MESH = pl.DeviceIdType.MESH
F32 = jnp.float32
BF16 = jnp.bfloat16
NX, NY, NZ = 4, 4, 8
ROWS = 80
LANES = 128
OWN, REST = 512, 384


def gelu_parts(pre_act):
    normal_cdf = 0.5 * (1.0 + lax.erf(pre_act * 0.7071067811865476))
    normal_pdf = jnp.exp(-0.5 * pre_act * pre_act) * 0.3989422804014327
    return (pre_act * normal_cdf, normal_cdf + pre_act * normal_pdf)


def swiglu_backward(gate_sum, up_sum, down_sum):
    logistic = jax.nn.sigmoid(gate_sum)
    swish_value = gate_sum * logistic
    swish_slope = logistic * (1.0 + gate_sum * (1.0 - logistic))
    hidden = (swish_value * up_sum).astype(BF16)
    gate_in = (down_sum * up_sum * swish_slope).astype(BF16)
    up_in = (down_sum * swish_value).astype(BF16)
    return (hidden, gate_in, up_in)


def dot(left, right):
    return jnp.dot(left, right, preferred_element_type=F32)


def dot_back(left, right):
    return lax.dot_general(left, right, (((1,), (1,)), ((), ())), preferred_element_type=F32)


def dot_tokens(left, right):
    return lax.dot_general(left, right, (((0,), (0,)), ((), ())), preferred_element_type=F32)


def at(start, size, unit):
    return pl.ds(pl.multiple_of(start, unit), size)


SCRATCH = dict(
    wi=((640, 160), BF16), wo=((160, 1024), BF16), wg=((1024, 896), BF16), wu=((1024, 896), BF16), wd=((896, 1024), BF16),
    pz=((128, 640), BF16), oz=((128, 1024), BF16), pf=((320, 640), BF16), of=((320, 1024), BF16),
    ap=((320, 160), BF16), ar=((3, ROWS, 160), BF16), a1=((ROWS, 160), BF16), a2=((ROWS, 160), BF16),
    slope=((ROWS, 160), F32), mh=((320, 160), BF16),
    mp=((320, 1024), BF16), my=((3, ROWS, 1024), BF16), ms=((ROWS, 1024), BF16), mz=((7, ROWS, LANES), BF16),
    m1=((ROWS, LANES), BF16), mf=((320, 1024), BF16),
    dp=((320, 896), BF16), dc=((320, OWN), BF16), d1=((320, OWN), BF16), dx=((3, ROWS, OWN), BF16),
    gp=((320, 896), BF16), gc=((320, OWN), BF16), g1=((320, OWN), BF16), gx=((3, ROWS, OWN), BF16),
    up=((320, 896), BF16), uc=((320, OWN), BF16), u1=((320, OWN), BF16), ux=((3, ROWS, OWN), BF16),
    dsum=((ROWS, OWN), F32),
    gio=((320, OWN), BF16), gir=((320, REST), BF16), uio=((320, OWN), BF16), uir=((320, REST), BF16),
    hdo=((320, OWN), BF16), hdr=((320, REST), BF16),
    bacc=((320, 1024), F32), bp=((320, 1024), BF16), by=((3, ROWS, 1024), BF16), bs=((ROWS, 1024), BF16),
    bz=((7, ROWS, LANES), BF16), b1=((ROWS, LANES), BF16), bf=((320, 1024), BF16),
    cp=((320, 160), BF16), cr=((3, ROWS, 160), BF16), c1=((ROWS, 160), BF16), c2=((ROWS, 160), BF16), pg=((320, 160), BF16),
    qp=((320, 640), BF16), qy=((3, ROWS, 640), BF16), qs=((ROWS, 640), BF16), qz=((7, ROWS, LANES), BF16),
    q1=((ROWS, LANES), BF16), qf=((320, 640), BF16),
    ig=((640, 160), BF16), og=((160, 1024), BF16), gg=((1024, 896), BF16), ug=((1024, 896), BF16), dg=((896, 1024), BF16),
)
SEMS = 128


class Refs:
    pass


def kernel(*refs):
    patches, grads, wi_in, wo_in, wg_in, wu_in, wd_in = refs[:7]
    pg_out, ig_out, og_out, gg_out, ug_out, dg_out = refs[7:13]
    s = Refs()
    for name, ref in zip(SCRATCH, refs[13:-3]):
        setattr(s, name, ref)
    send_sems, recv_sems, local_sems = refs[-3:]
    gx, gy, gz = lax.axis_index("gx"), lax.axis_index("gy"), lax.axis_index("gz")
    x, c = gx // 2, gx % 2
    y, z = gy // 2, (gy % 2) * 4 + gz
    to_y = [((y + d) % NY, (gx, ((y + d) % NY) * 2 + z // 4, gz)) for d in (1, 3, 2)]
    to_x = [((x + d) % NX, (((x + d) % NX) * 2 + c, gy, gz)) for d in (1, 3, 2)]
    to_z = [((z + d) % NZ, (gx, y * 2 + ((z + d) % NZ) // 4, ((z + d) % NZ) % 4)) for d in (4, 3, 5, 2, 6, 1, 7)]
    to_c = (x * 2 + (1 - c), gy, gz)

    started = []
    count = [0, 0]

    def send(src, dst, device):
        i = count[0]
        count[0] += 1
        copy = pltpu.make_async_remote_copy(
            src_ref=src, dst_ref=dst, send_sem=send_sems.at[i], recv_sem=recv_sems.at[i], device_id=device, device_id_type=MESH
        )
        copy.start()
        started.append(copy.wait_send)
        return copy

    def move(src, dst):
        copy = pltpu.make_async_copy(src, dst, local_sems.at[count[1]])
        count[1] += 1
        copy.start()
        return copy

    def arrive(copies):
        for copy in copies:
            copy.wait_recv()

    def rows(i):
        return at(i * ROWS, ROWS, 16)

    def cols(i):
        return at(i * LANES, LANES, LANES)

    def scatter_rows(src, dst, peers):
        return [send(src.at[rows(p)], dst.at[k], device) for k, (p, device) in enumerate(peers)]

    def gather_rows(buf, me, peers):
        return [send(buf.at[rows(me)], buf.at[rows(me)], device) for _, device in peers]

    def scatter_cols(src, dst):
        return [send(src.at[:, cols(p)], dst.at[k], device) for k, (p, device) in enumerate(to_z)]

    def gather_cols(src, buf):
        return [send(src, buf.at[rows(y), cols(z)], device) for _, device in to_z]

    def total(own, parts):
        value = own.astype(F32)
        for k in range(parts.shape[0]):
            value = value + parts[k].astype(F32)
        return value

    loads = {n: move(r, getattr(s, n)) for n, r in (("wi", wi_in), ("wo", wo_in), ("wd", wd_in), ("wg", wg_in), ("wu", wu_in))}

    barrier = pltpu.get_barrier_semaphore()
    peers = [d for _, d in to_y + to_x + to_z] + [to_c]
    for device in peers:
        pl.semaphore_signal(barrier, inc=1, device_id=device, device_id_type=MESH)
    pl.semaphore_wait(barrier, len(peers))

    def gather_z(src, buf):
        copies = [send(src, buf.at[at(z * 16, 16, 16)], device) for _, device in to_z]
        buf[at(z * 16, 16, 16), :] = src[...]
        return copies

    row = lax.broadcasted_iota(jnp.int32, (ROWS, 128), 0)
    col = lax.broadcasted_iota(jnp.int32, (ROWS, 128), 1)
    pick = jnp.where(col == row + 6 * ((row * 205) >> 11), 1.0, 0.0).astype(BF16)

    p_z = gather_z(patches, s.pz)
    arrive(p_z)
    s.pf[rows(y), :] = dot(pick, s.pz[...]).astype(BF16)
    p_y = gather_rows(s.pf, y, to_y)
    o_z = gather_z(grads, s.oz)
    loads["wi"].wait()
    arrive(p_y)

    s.ap[...] = dot(s.pf[...], s.wi[...]).astype(BF16)
    a_x = scatter_rows(s.ap, s.ar, to_x)
    arrive(o_z)
    s.of[rows(y), :] = dot(pick, s.oz[...]).astype(BF16)
    o_y = gather_rows(s.of, y, to_y)
    arrive(a_x)
    s.a1[...] = total(s.ap[rows(x), :], s.ar).astype(BF16)
    a_c = send(s.a1, s.a2, to_c)
    a_c.wait_recv()
    gelu_value, gelu_slope = gelu_parts(s.a1[...].astype(F32) + s.a2[...].astype(F32))
    s.mh[rows(x), :] = gelu_value.astype(BF16)
    h_x = gather_rows(s.mh, x, to_x)
    s.slope[...] = gelu_slope
    loads["wo"].wait()
    arrive(h_x)

    s.mp[...] = dot(s.mh[...], s.wo[...]).astype(BF16)
    m_y = scatter_rows(s.mp, s.my, to_y)
    loads["wd"].wait()
    arrive(o_y)

    def tiles(total_cols, fn):
        full = total_cols // 256

        def step(t, carry):
            fn(pl.multiple_of(t * 256, 256), 256)
            return carry

        lax.fori_loop(0, full, step, 0)
        if total_cols % 256:
            fn(full * 256, total_cols % 256)

    def down_tile(start, size):
        s.dp[:, pl.ds(start, size)] = dot_back(s.of[...], s.wd[pl.ds(start, size), :]).astype(BF16)

    tiles(896, down_tile)
    mine = at(c * REST, OWN, LANES)
    theirs = at((1 - c) * REST, OWN, LANES)
    d_c = send(s.dp.at[:, theirs], s.dc, to_c)
    arrive(m_y)
    s.ms[...] = total(s.mp[rows(y), :], s.my).astype(BF16)
    m_z = scatter_cols(s.ms, s.mz)
    d_c.wait_recv()
    s.d1[...] = (s.dp[:, mine].astype(F32) + s.dc[...].astype(F32)).astype(BF16)
    d_x = scatter_rows(s.d1, s.dx, to_x)
    arrive(m_z)
    s.m1[...] = total(s.ms[:, cols(z)], s.mz).astype(BF16)
    m_gz = gather_cols(s.m1, s.mf)
    s.mf[rows(y), cols(z)] = s.m1[...]
    arrive(m_gz)
    m_gy = gather_rows(s.mf, y, to_y)
    arrive(d_x)
    s.dsum[...] = total(s.d1[rows(x), :], s.dx)
    loads["wg"].wait()
    loads["wu"].wait()
    arrive(m_gy)

    def gate_tile(start, size):
        s.gp[:, pl.ds(start, size)] = dot(s.mf[...], s.wg[:, pl.ds(start, size)]).astype(BF16)

    def up_tile(start, size):
        s.up[:, pl.ds(start, size)] = dot(s.mf[...], s.wu[:, pl.ds(start, size)]).astype(BF16)

    tiles(896, gate_tile)
    g_c = send(s.gp.at[:, theirs], s.gc, to_c)
    tiles(896, up_tile)
    u_c = send(s.up.at[:, theirs], s.uc, to_c)
    g_c.wait_recv()
    s.g1[...] = (s.gp[:, mine].astype(F32) + s.gc[...].astype(F32)).astype(BF16)
    g_x = scatter_rows(s.g1, s.gx, to_x)
    u_c.wait_recv()
    s.u1[...] = (s.up[:, mine].astype(F32) + s.uc[...].astype(F32)).astype(BF16)
    u_x = scatter_rows(s.u1, s.ux, to_x)
    arrive(g_x)
    arrive(u_x)
    hidden, gate_in, up_in = swiglu_backward(total(s.g1[rows(x), :], s.gx), total(s.u1[rows(x), :], s.ux), s.dsum[...])
    s.gio[rows(x), :] = gate_in
    gi_x = gather_rows(s.gio, x, to_x)
    s.uio[rows(x), :] = up_in
    ui_x = gather_rows(s.uio, x, to_x)
    s.hdo[rows(x), :] = hidden
    hd_x = gather_rows(s.hdo, x, to_x)

    give = at(c * LANES, REST, LANES)
    rest = at((1 - c) * OWN, REST, LANES)
    arrive(gi_x)
    gi_c = send(s.gio.at[:, give], s.gir, to_c)

    def back_gate(start, size):
        s.bacc[:, pl.ds(start, size)] = dot_back(s.gio[...], s.wg[pl.ds(start, size), mine])

    tiles(1024, back_gate)
    arrive(ui_x)
    ui_c = send(s.uio.at[:, give], s.uir, to_c)
    gi_c.wait_recv()

    def back_mid(start, size):
        s.bacc[:, pl.ds(start, size)] += dot_back(s.uio[...], s.wu[pl.ds(start, size), mine]) + dot_back(
            s.gir[...], s.wg[pl.ds(start, size), rest]
        )

    tiles(1024, back_mid)
    ui_c.wait_recv()

    def back_last(start, size):
        s.bp[:, pl.ds(start, size)] = (
            s.bacc[:, pl.ds(start, size)] + dot_back(s.uir[...], s.wu[pl.ds(start, size), rest])
        ).astype(BF16)

    tiles(1024, back_last)
    b_y = scatter_rows(s.bp, s.by, to_y)
    stores = []

    def gate_grad(start, size):
        left = s.mf[:, pl.ds(start, size)]
        s.gg[pl.ds(start, size), mine] = dot_tokens(left, s.gio[...]).astype(BF16)
        s.gg[pl.ds(start, size), rest] = dot_tokens(left, s.gir[...]).astype(BF16)

    def up_grad(start, size):
        left = s.mf[:, pl.ds(start, size)]
        s.ug[pl.ds(start, size), mine] = dot_tokens(left, s.uio[...]).astype(BF16)
        s.ug[pl.ds(start, size), rest] = dot_tokens(left, s.uir[...]).astype(BF16)

    arrive(hd_x)
    hd_c = send(s.hdo.at[:, give], s.hdr, to_c)
    tiles(1024, gate_grad)
    stores.append(move(s.gg, gg_out))
    arrive(b_y)
    s.bs[...] = total(s.bp[rows(y), :], s.by).astype(BF16)
    b_z = scatter_cols(s.bs, s.bz)
    tiles(1024, up_grad)
    stores.append(move(s.ug, ug_out))
    arrive(b_z)
    back_sum = total(s.bs[:, cols(z)], s.bz)
    s.b1[...] = (s.of[rows(y), cols(z)].astype(F32) + back_sum).astype(BF16)
    b_gz = gather_cols(s.b1, s.bf)
    s.bf[rows(y), cols(z)] = s.b1[...]
    hd_c.wait_recv()

    def down_grad(start, size):
        right = s.of[:, pl.ds(start, size)]
        s.dg[mine, pl.ds(start, size)] = dot_tokens(s.hdo[...], right).astype(BF16)
        s.dg[rest, pl.ds(start, size)] = dot_tokens(s.hdr[...], right).astype(BF16)

    tiles(1024, down_grad)
    stores.append(move(s.dg, dg_out))
    arrive(b_gz)
    b_gy = gather_rows(s.bf, y, to_y)
    arrive(b_gy)

    s.cp[...] = dot_back(s.bf[...], s.wo[...]).astype(BF16)
    c_x = scatter_rows(s.cp, s.cr, to_x)
    s.og[...] = dot_tokens(s.mh[...], s.bf[...]).astype(BF16)
    stores.append(move(s.og, og_out))
    arrive(c_x)
    s.c1[...] = total(s.cp[rows(x), :], s.cr).astype(BF16)
    c_c = send(s.c1, s.c2, to_c)
    c_c.wait_recv()
    act_grad = s.c1[...].astype(F32) + s.c2[...].astype(F32)
    s.pg[rows(x), :] = (act_grad * s.slope[...]).astype(BF16)
    p_x = gather_rows(s.pg, x, to_x)
    arrive(p_x)

    s.qp[...] = dot_back(s.pg[...], s.wi[...]).astype(BF16)
    q_y = scatter_rows(s.qp, s.qy, to_y)
    s.ig[...] = dot_tokens(s.pf[...], s.pg[...]).astype(BF16)
    stores.append(move(s.ig, ig_out))
    arrive(q_y)
    s.qs[...] = total(s.qp[rows(y), :], s.qy).astype(BF16)

    def plan(src, dst, device):
        i = count[0]
        count[0] += 1
        return pltpu.make_async_remote_copy(
            src_ref=src, dst_ref=dst, send_sem=send_sems.at[i], recv_sem=recv_sems.at[i], device_id=device, device_id_type=MESH
        )

    owners = 5
    last = [(p, plan(s.qs.at[:, cols(jnp.minimum(p, owners - 1))], s.qz.at[k], device)) for k, (p, device) in enumerate(to_z)]
    for p, copy in last:
        pl.when(p < owners)(copy.start)
    zc = cols(jnp.minimum(z, owners - 1))
    spread = [plan(s.q1, s.qf.at[rows(y), zc], device) for _, device in to_z]

    @pl.when(z < owners)
    def _():
        for _, copy in last:
            copy.wait_recv()
        s.q1[...] = total(s.qs[:, zc], s.qz).astype(BF16)
        for copy in spread:
            copy.start()
        s.qf[rows(y), zc] = s.q1[...]

    for copy, d in zip(spread, (4, 3, 5, 2, 6, 1, 7)):
        pl.when((z + NZ - d) % NZ < owners)(copy.wait_recv)
    q_gy = gather_rows(s.qf, y, to_y)
    arrive(q_gy)
    stores.append(move(s.qf, pg_out))

    for wait_send in started:
        wait_send()
    for p, copy in last:
        pl.when(p < owners)(copy.wait_send)

    @pl.when(z < owners)
    def _():
        for copy in spread:
            copy.wait_send()

    for copy in stores:
        copy.wait()


def local(patches, merge_inner, merge_outer, gate_weight, up_weight, down_weight, out_grad):
    pad = ((0, 6), (0, 0))
    anywhere = pl.BlockSpec(memory_space=pl.ANY)
    vmem = pl.BlockSpec(memory_space=pltpu.VMEM)
    shapes = [(320, 640), (640, 160), (160, 1024), (1024, 896), (1024, 896), (896, 1024)]
    return pl.pallas_call(
        kernel,
        out_shape=[jax.ShapeDtypeStruct(shape, BF16) for shape in shapes],
        in_specs=[vmem] * 2 + [anywhere] * 5,
        out_specs=[anywhere] * 6,
        scratch_shapes=[pltpu.VMEM(shape, dtype) for shape, dtype in SCRATCH.values()]
        + [pltpu.SemaphoreType.DMA((SEMS,)), pltpu.SemaphoreType.DMA((SEMS,)), pltpu.SemaphoreType.DMA((16,))],
        compiler_params=pltpu.CompilerParams(collective_id=0, has_side_effects=True, vmem_limit_bytes=56 * 2**20),
    )(jnp.pad(patches, pad), jnp.pad(out_grad, pad), merge_inner, merge_outer, gate_weight, up_weight, down_weight)


def solution(mesh):
    in_specs = (
        P(("gy", "gz"), "gx"),
        P("gx", ("gy", "gz")),
        P(("gy", "gz"), "gx"),
        P("gx", ("gy", "gz")),
        P("gx", ("gy", "gz")),
        P(("gy", "gz"), "gx"),
        P(("gy", "gz"), "gx"),
    )
    out_specs = (
        P(None, "gx"),
        P("gx", ("gy", "gz")),
        P(("gy", "gz"), "gx"),
        P("gx", ("gy", "gz")),
        P("gx", ("gy", "gz")),
        P(("gy", "gz"), "gx"),
    )
    return jax.shard_map(local, mesh=mesh, in_specs=in_specs, out_specs=out_specs, check_vma=False)
```

```python
import jax
import jax.numpy as jnp
from jax import lax
from jax.experimental import pallas as pl
from jax.experimental.pallas import tpu as pltpu
from jax.sharding import PartitionSpec as P

MESH = pl.DeviceIdType.MESH
F32 = jnp.float32
BF16 = jnp.bfloat16
NX, NY, NZ = 4, 4, 8
ROWS = 80
LANES = 128
OWN, REST = 512, 384


def gelu_parts(pre_act):
    normal_cdf = 0.5 * (1.0 + lax.erf(pre_act * 0.7071067811865476))
    normal_pdf = jnp.exp(-0.5 * pre_act * pre_act) * 0.3989422804014327
    return (pre_act * normal_cdf, normal_cdf + pre_act * normal_pdf)


def swiglu_backward(gate_sum, up_sum, down_sum):
    logistic = jax.nn.sigmoid(gate_sum)
    swish_value = gate_sum * logistic
    swish_slope = logistic * (1.0 + gate_sum * (1.0 - logistic))
    hidden = (swish_value * up_sum).astype(BF16)
    gate_in = (down_sum * up_sum * swish_slope).astype(BF16)
    up_in = (down_sum * swish_value).astype(BF16)
    return (hidden, gate_in, up_in)


def dot(left, right):
    return jnp.dot(left, right, preferred_element_type=F32)


def dot_back(left, right):
    return lax.dot_general(left, right, (((1,), (1,)), ((), ())), preferred_element_type=F32)


def dot_tokens(left, right):
    return lax.dot_general(left, right, (((0,), (0,)), ((), ())), preferred_element_type=F32)


def at(start, size, unit):
    return pl.ds(pl.multiple_of(start, unit), size)


SCRATCH = dict(
    wi=((640, 640), BF16), wo=((640, 1024), BF16), wg=((1024, 896), BF16), wu=((1024, 896), BF16), wd=((896, 1024), BF16),
    p10=((10, 640), BF16), o10=((10, 1024), BF16), pp=((16, 640), BF16), op=((16, 1024), BF16),
    pz=((128, 640), BF16), oz=((128, 1024), BF16), pf=((320, 640), BF16), of=((320, 1024), BF16),
    ax=((NX, ROWS, 640), BF16), a1=((ROWS, 640), BF16), a2=((ROWS, 640), BF16), slope=((ROWS, 640), F32),
    hs=((NY, ROWS, 160), BF16), hr=((NY, ROWS, 160), BF16),
    ms=((ROWS, 1024), BF16), mz=((7, ROWS, LANES), BF16), m1=((ROWS, LANES), BF16), mf=((NY, ROWS, 1024), BF16),
    dp=((320, 896), BF16), dc=((320, OWN), BF16), d1=((320, OWN), BF16), dx=((3, ROWS, OWN), BF16),
    gp=((320, 896), BF16), gc=((320, OWN), BF16), g1=((320, OWN), BF16), gx=((3, ROWS, OWN), BF16),
    up=((320, 896), BF16), uc=((320, OWN), BF16), u1=((320, OWN), BF16), ux=((3, ROWS, OWN), BF16),
    dsum=((ROWS, OWN), F32),
    gio=((320, OWN), BF16), gir=((320, REST), BF16), uio=((320, OWN), BF16), uir=((320, REST), BF16),
    hdo=((320, OWN), BF16), hdr=((320, REST), BF16),
    bacc=((320, 1024), F32), bp=((320, 1024), BF16), by=((3, ROWS, 1024), BF16), bs=((ROWS, 1024), BF16),
    bz=((7, ROWS, LANES), BF16), b1=((ROWS, LANES), BF16), bf=((NY, ROWS, 1024), BF16),
    cx=((NX, ROWS, 640), BF16), c1=((ROWS, 640), BF16), c2=((ROWS, 640), BF16), pg=((ROWS, 640), BF16),
    gs=((NY, ROWS, 160), BF16), gr=((NY, ROWS, 160), BF16),
    qs=((ROWS, 640), BF16), qz=((7, ROWS, LANES), BF16), q1=((ROWS, LANES), BF16),
)
SEMS = 192
FIRST = 48
OWNERS = 5


class Refs:
    pass


def kernel(*refs):
    patches, grads, wi_in, wo_in, wg_in, wu_in, wd_in = refs[:7]
    s = Refs()
    s.qf, s.ig, s.og, s.gg, s.ug, s.dg = refs[7:13]
    for name, ref in zip(SCRATCH, refs[13:-3]):
        setattr(s, name, ref)
    send_sems, recv_sems, local_sems = refs[-3:]
    gx, gy, gz = lax.axis_index("gx"), lax.axis_index("gy"), lax.axis_index("gz")
    x, c = gx // 2, gx % 2
    y, z = gy // 2, (gy % 2) * 4 + gz
    ring = (1, 3, 2)
    ring_z = (4, 3, 5, 2, 6, 1, 7)
    to_y = [((y + d) % NY, (gx, ((y + d) % NY) * 2 + z // 4, gz)) for d in ring]
    to_x = [((x + d) % NX, (((x + d) % NX) * 2 + c, gy, gz)) for d in ring]
    to_z = [((z + d) % NZ, (gx, y * 2 + ((z + d) % NZ) // 4, ((z + d) % NZ) % 4)) for d in ring_z]
    to_c = (x * 2 + (1 - c), gy, gz)

    started = []
    count = [0, 0]

    def plan(src, dst, device):
        i = count[0]
        count[0] += 1
        return pltpu.make_async_remote_copy(
            src_ref=src, dst_ref=dst, send_sem=send_sems.at[i], recv_sem=recv_sems.at[i], device_id=device, device_id_type=MESH
        )

    def send(src, dst, device):
        copy = plan(src, dst, device)
        copy.start()
        started.append(copy.wait_send)
        return copy

    def move(src, dst):
        copy = pltpu.make_async_copy(src, dst, local_sems.at[count[1]])
        count[1] += 1
        copy.start()
        return copy

    def arrive(copies):
        for copy in copies:
            copy.wait_recv()

    def rows(i):
        return at(i * ROWS, ROWS, 16)

    def cols(i):
        return at(i * LANES, LANES, LANES)

    def scatter_rows(src, dst, peers, part=slice(None)):
        return [send(src.at[rows(p), part], dst.at[k, :, part], device) for k, (p, device) in enumerate(peers)]

    def spread(ref, peers):
        return [send(ref, ref, device) for _, device in peers]

    def scatter_cols(src, dst):
        return [send(src.at[:, cols(p)], dst.at[k], device) for k, (p, device) in enumerate(to_z)]

    def total(own, parts):
        value = own.astype(F32)
        for k in range(parts.shape[0]):
            value = value + parts[k].astype(F32)
        return value

    def in_order(parts):
        return total(parts[0], parts.at[1:])

    def tiles(total_cols, fn):
        full = total_cols // 256

        def step(t, carry):
            fn(pl.multiple_of(t * 256, 256), 256)
            return carry

        lax.fori_loop(0, full, step, 0)
        if total_cols % 256:
            fn(full * 256, total_cols % 256)

    strip = at(y * 160, 160, 16)
    loads = {n: move(r, d) for n, r, d in (
        ("patches", patches, s.p10), ("grads", grads, s.o10),
        ("wi", wi_in, s.wi.at[strip]), ("wo", wo_in, s.wo.at[strip]), ("wd", wd_in, s.wd), ("wg", wg_in, s.wg), ("wu", wu_in, s.wu)
    )}

    barrier = pltpu.get_barrier_semaphore()
    peers = [d for _, d in to_z + to_y + to_x] + [to_c]
    for device in peers:
        pl.semaphore_signal(barrier, inc=1, device_id=device, device_id_type=MESH)

    deal = (lax.broadcasted_iota(jnp.int32, (16, 10), 0) == lax.broadcasted_iota(jnp.int32, (16, 10), 1)).astype(F32).astype(BF16)
    loads["patches"].wait()
    s.pp[...] = dot(deal, s.p10[...]).astype(BF16)
    loads["grads"].wait()
    s.op[...] = dot(deal, s.o10[...]).astype(BF16)
    row = lax.broadcasted_iota(jnp.int32, (ROWS, 128), 0)
    col = lax.broadcasted_iota(jnp.int32, (ROWS, 128), 1)
    pick = jnp.where(col == row + 6 * ((row * 205) >> 11), 1.0, 0.0).astype(BF16)
    pl.semaphore_wait(barrier, len(peers))

    def gather_z(src, buf):
        copies = [send(src, buf.at[at(z * 16, 16, 16)], device) for _, device in to_z]
        buf[at(z * 16, 16, 16), :] = src[...]
        return copies

    p_z = gather_z(s.pp, s.pz)
    wi_y = [send(wi_in, s.wi.at[strip], device) for _, device in to_y]
    arrive(p_z)
    wo_y = [send(wo_in, s.wo.at[strip], device) for _, device in to_y]
    o_z = gather_z(s.op, s.oz)
    block = dot(pick, s.pz[...]).astype(BF16)
    s.pf[rows(y), :] = block
    loads["wi"].wait()
    arrive(wi_y)

    s.ax[x] = dot_back(block, s.wi[...]).astype(BF16)
    a_x = spread(s.ax.at[x], to_x)
    arrive(o_z)
    s.of[rows(y), :] = dot(pick, s.oz[...]).astype(BF16)
    arrive(a_x)
    s.a1[...] = in_order(s.ax).astype(BF16)
    a_c = send(s.a1, s.a2, to_c)
    arrive([a_c])
    gelu_value, gelu_slope = gelu_parts(s.a1[...].astype(F32) + s.a2[...].astype(F32))
    loads["wo"].wait()
    arrive(wo_y)

    s.ms[...] = dot(gelu_value.astype(BF16), s.wo[...]).astype(BF16)
    m_z = scatter_cols(s.ms, s.mz)
    o_y = spread(s.of.at[rows(y)], to_y)
    s.slope[...] = gelu_slope

    def deal_out(value, src, dst):
        for q in range(NY):
            src[q] = value[:, q * 160 : (q + 1) * 160].astype(BF16)
        dst[y] = src[y]
        return [send(src.at[p], dst.at[y], device) for p, device in to_y]

    h_y = deal_out(gelu_value, s.hs, s.hr)
    loads["wd"].wait()
    arrive(m_z)
    s.m1[...] = total(s.ms[:, cols(z)], s.mz).astype(BF16)
    s.mf[y, :, cols(z)] = s.m1[...]
    first, second = pl.ds(0, FIRST), pl.ds(FIRST, ROWS - FIRST)
    m_z1 = [send(s.m1.at[first], s.mf.at[y, first, cols(z)], device) for _, device in to_z]
    m_y2 = [send(s.m1.at[second], s.mf.at[y, second, cols(z)], device) for _, device in to_y]
    arrive(m_y2)
    m_z2 = spread(s.mf.at[:, second, cols(z)], to_z)
    arrive(m_z1)
    m_y1 = spread(s.mf.at[y, first], to_y)
    arrive(o_y)

    def down_tile(start, size):
        s.dp[:, pl.ds(start, size)] = dot_back(s.of[...], s.wd[pl.ds(start, size), :]).astype(BF16)

    tiles(896, down_tile)
    mine = at(c * REST, OWN, LANES)
    theirs = at((1 - c) * REST, OWN, LANES)
    d_c = send(s.dp.at[:, theirs], s.dc, to_c)
    loads["wg"].wait()
    loads["wu"].wait()
    arrive([d_c])
    s.d1[...] = (s.dp[:, mine].astype(F32) + s.dc[...].astype(F32)).astype(BF16)
    d_x = scatter_rows(s.d1, s.dx, to_x)
    arrive(m_z2)
    arrive(m_y1)
    merged = s.mf.reshape(320, 1024)

    def gate_tile(start, size):
        s.gp[:, pl.ds(start, size)] = dot(merged[...], s.wg[:, pl.ds(start, size)]).astype(BF16)

    def up_tile(start, size):
        s.up[:, pl.ds(start, size)] = dot(merged[...], s.wu[:, pl.ds(start, size)]).astype(BF16)

    tiles(896, gate_tile)
    g_c = send(s.gp.at[:, theirs], s.gc, to_c)
    tiles(896, up_tile)
    u_c = send(s.up.at[:, theirs], s.uc, to_c)
    arrive([g_c])
    s.g1[...] = (s.gp[:, mine].astype(F32) + s.gc[...].astype(F32)).astype(BF16)
    g_x = scatter_rows(s.g1, s.gx, to_x)
    arrive([u_c])
    s.u1[...] = (s.up[:, mine].astype(F32) + s.uc[...].astype(F32)).astype(BF16)
    u_x = scatter_rows(s.u1, s.ux, to_x)
    p_y = spread(s.pf.at[rows(y)], to_y)
    arrive(d_x)
    s.dsum[...] = total(s.d1[rows(x), :], s.dx)
    arrive(g_x)
    arrive(u_x)
    hidden, gate_in, up_in = swiglu_backward(total(s.g1[rows(x), :], s.gx), total(s.u1[rows(x), :], s.ux), s.dsum[...])
    give = at(c * LANES, REST, LANES)
    rest = at((1 - c) * OWN, REST, LANES)

    def gather_x(value, buf, other):
        buf[rows(x), :] = value
        copies = spread(buf.at[rows(x)], to_x)
        return copies, [send(buf.at[rows(x), give], other.at[rows(x)], to_c)]

    def hand_over(copies, given, buf, other):
        for copy, d in zip(copies, ring):
            arrive([copy])
            p = rows((x + NX - d) % NX)
            given.append(send(buf.at[p, give], other.at[p], to_c))

    gi_x, gi_c = gather_x(gate_in, s.gio, s.gir)
    ui_x, ui_c = gather_x(up_in, s.uio, s.uir)
    hd_x, hd_c = gather_x(hidden, s.hdo, s.hdr)

    hand_over(gi_x, gi_c, s.gio, s.gir)

    def back_gate(start, size):
        s.bacc[:, pl.ds(start, size)] = dot_back(s.gio[...], s.wg[pl.ds(start, size), mine])

    tiles(1024, back_gate)
    hand_over(ui_x, ui_c, s.uio, s.uir)
    arrive(gi_c)

    def back_mid(start, size):
        s.bacc[:, pl.ds(start, size)] += dot_back(s.uio[...], s.wu[pl.ds(start, size), mine]) + dot_back(
            s.gir[...], s.wg[pl.ds(start, size), rest]
        )

    tiles(1024, back_mid)
    arrive(ui_c)
    b_y = []
    for t in range(4):
        part = pl.ds(t * 256, 256)
        s.bp[:, part] = (s.bacc[:, part] + dot_back(s.uir[...], s.wu[part, rest])).astype(BF16)
        b_y += scatter_rows(s.bp, s.by, to_y, part)

    def gate_grad(start, size):
        left = merged[:, pl.ds(start, size)]
        s.gg[pl.ds(start, size), mine] = dot_tokens(left, s.gio[...]).astype(BF16)
        s.gg[pl.ds(start, size), rest] = dot_tokens(left, s.gir[...]).astype(BF16)

    def up_grad(start, size):
        left = merged[:, pl.ds(start, size)]
        s.ug[pl.ds(start, size), mine] = dot_tokens(left, s.uio[...]).astype(BF16)
        s.ug[pl.ds(start, size), rest] = dot_tokens(left, s.uir[...]).astype(BF16)

    hand_over(hd_x, hd_c, s.hdo, s.hdr)
    tiles(1024, gate_grad)
    arrive(b_y)
    s.bs[...] = total(s.bp[rows(y), :], s.by).astype(BF16)
    b_z = scatter_cols(s.bs, s.bz)
    tiles(1024, up_grad)
    arrive(b_z)
    s.b1[...] = (s.of[rows(y), cols(z)].astype(F32) + total(s.bs[:, cols(z)], s.bz)).astype(BF16)
    s.bf[y, :, cols(z)] = s.b1[...]
    b_gz = [send(s.b1, s.bf.at[y, :, cols(z)], device) for _, device in to_z]
    arrive(hd_c)

    def down_grad(start, size):
        right = s.of[:, pl.ds(start, size)]
        s.dg[mine, pl.ds(start, size)] = dot_tokens(s.hdo[...], right).astype(BF16)
        s.dg[rest, pl.ds(start, size)] = dot_tokens(s.hdr[...], right).astype(BF16)

    tiles(1024, down_grad)
    arrive(b_gz)

    s.cx[x] = dot_back(s.bf[y], s.wo[...]).astype(BF16)
    c_x = spread(s.cx.at[x], to_x)
    b_gy = spread(s.bf.at[y], to_y)
    arrive(h_y)
    arrive(p_y)
    arrive(c_x)
    s.c1[...] = in_order(s.cx).astype(BF16)
    c_c = send(s.c1, s.c2, to_c)
    arrive([c_c])
    pre_grad = (s.c1[...].astype(F32) + s.c2[...].astype(F32)) * s.slope[...]
    s.pg[...] = pre_grad.astype(BF16)

    s.qs[...] = dot(s.pg[...], s.wi[...]).astype(BF16)
    owner = z < OWNERS
    zc = cols(jnp.minimum(z, OWNERS - 1))
    q_z = [(p, plan(s.qs.at[:, cols(jnp.minimum(p, OWNERS - 1))], s.qz.at[k], device)) for k, (p, device) in enumerate(to_z)]
    for p, copy in q_z:
        pl.when(p < OWNERS)(copy.start)
    g_y = deal_out(pre_grad, s.gs, s.gr)
    arrive(b_gy)
    s.og[...] = dot_tokens(s.hr.reshape(320, 160)[...], s.bf.reshape(320, 1024)[...]).astype(BF16)
    q_z1 = [plan(s.q1.at[first], s.qf.at[y, first, zc], device) for _, device in to_z]
    q_y2 = [plan(s.q1.at[second], s.qf.at[y, second, zc], device) for _, device in to_y]
    q_z2 = [plan(s.qf.at[:, second, zc], s.qf.at[:, second, zc], device) for _, device in to_z]

    @pl.when(owner)
    def _():
        for _, copy in q_z:
            copy.wait_recv()
        s.q1[...] = total(s.qs[:, zc], s.qz).astype(BF16)
        s.qf[y, :, zc] = s.q1[...]
        for copy in q_z1 + q_y2:
            copy.start()
        arrive(q_y2)
        for copy in q_z2:
            copy.start()

    sources = [(z + NZ - d) % NZ < OWNERS for d in ring_z]
    for copy, sends in zip(q_z1, sources):
        pl.when(sends)(copy.wait_recv)
    q_y1 = spread(s.qf.at[y, first], to_y)
    arrive(g_y)
    s.ig[...] = dot_tokens(s.gr.reshape(320, 160)[...], s.pf[...]).astype(BF16)
    for copy, sends in zip(q_z2, sources):
        pl.when(sends)(copy.wait_recv)
    arrive(q_y1)

    for wait_send in started:
        wait_send()
    for p, copy in q_z:
        pl.when(p < OWNERS)(copy.wait_send)

    @pl.when(owner)
    def _():
        for copy in q_z1 + q_y2 + q_z2:
            copy.wait_send()


def local(patches, merge_inner, merge_outer, gate_weight, up_weight, down_weight, out_grad):
    vmem = pl.BlockSpec(memory_space=pltpu.VMEM)
    in_hbm = pl.BlockSpec(memory_space=pltpu.HBM)
    shapes = [(NY, ROWS, 640), (160, 640), (160, 1024), (1024, 896), (1024, 896), (896, 1024)]
    arrays = (patches, out_grad, merge_inner.T, merge_outer, gate_weight, up_weight, down_weight)
    results = pl.pallas_call(
        kernel,
        out_shape=[pltpu.VMEM(shape, BF16) for shape in shapes],
        in_specs=[in_hbm] * 7,
        out_specs=[vmem] * 6,
        scratch_shapes=[pltpu.VMEM(shape, dtype) for shape, dtype in SCRATCH.values()]
        + [pltpu.SemaphoreType.DMA((SEMS,)), pltpu.SemaphoreType.DMA((SEMS,)), pltpu.SemaphoreType.DMA((16,))],
        compiler_params=pltpu.CompilerParams(collective_id=0, has_side_effects=True, vmem_limit_bytes=56 * 2**20),
        name="layer",
    )(*(pltpu.with_memory_space_constraint(a, pltpu.HBM) for a in arrays))
    patch_grad, inner_grad, *others = results
    return (patch_grad.reshape(320, 640), inner_grad.T, *others)


def solution(mesh):
    in_specs = (
        P(("gy", "gz"), "gx"),
        P("gx", ("gy", "gz")),
        P(("gy", "gz"), "gx"),
        P("gx", ("gy", "gz")),
        P("gx", ("gy", "gz")),
        P(("gy", "gz"), "gx"),
        P(("gy", "gz"), "gx"),
    )
    out_specs = (
        P(None, "gx"),
        P("gx", ("gy", "gz")),
        P(("gy", "gz"), "gx"),
        P("gx", ("gy", "gz")),
        P("gx", ("gy", "gz")),
        P(("gy", "gz"), "gx"),
    )
    return jax.shard_map(local, mesh=mesh, in_specs=in_specs, out_specs=out_specs, check_vma=False)
```

```python
import jax
import jax.numpy as jnp
from jax import lax
from jax.experimental import pallas as pl
from jax.experimental.pallas import tpu as pltpu
from jax.sharding import PartitionSpec as P

MESH = pl.DeviceIdType.MESH
F32 = jnp.float32
BF16 = jnp.bfloat16
NX, NY, NZ = 4, 4, 8
ROWS = 80
LANES = 128
OWN, REST = 512, 384


def gelu_parts(pre_act):
    normal_cdf = 0.5 * (1.0 + lax.erf(pre_act * 0.7071067811865476))
    normal_pdf = jnp.exp(-0.5 * pre_act * pre_act) * 0.3989422804014327
    return (pre_act * normal_cdf, normal_cdf + pre_act * normal_pdf)


def swiglu_backward(gate_sum, up_sum, down_sum):
    logistic = jax.nn.sigmoid(gate_sum)
    swish_value = gate_sum * logistic
    swish_slope = logistic * (1.0 + gate_sum * (1.0 - logistic))
    hidden = (swish_value * up_sum).astype(BF16)
    gate_in = (down_sum * up_sum * swish_slope).astype(BF16)
    up_in = (down_sum * swish_value).astype(BF16)
    return (hidden, gate_in, up_in)


def dot(left, right):
    return jnp.dot(left, right, preferred_element_type=F32)


def dot_back(left, right):
    return lax.dot_general(left, right, (((1,), (1,)), ((), ())), preferred_element_type=F32)


def dot_tokens(left, right):
    return lax.dot_general(left, right, (((0,), (0,)), ((), ())), preferred_element_type=F32)


def at(start, size, unit):
    return pl.ds(pl.multiple_of(start, unit), size)


SCRATCH = dict(
    wi=((640, 640), BF16), wo=((640, 1024), BF16), wg=((1024, 896), BF16), wu=((1024, 896), BF16), wd=((896, 1024), BF16),
    p10=((10, 640), BF16), o10=((10, 1024), BF16), pp=((16, 640), BF16), op=((16, 1024), BF16),
    pz=((128, 640), BF16), oz=((128, 1024), BF16), pf=((NY, ROWS, 640), BF16), of=((NY, ROWS, 1024), BF16),
    dp=((NX, ROWS, 896), BF16), dc=((NX, ROWS, OWN), BF16), d1=((NX, ROWS, OWN), BF16), dx=((3, ROWS, OWN), BF16),
    dsum=((ROWS, OWN), F32),
)
PARTS = ((0, 48), (48, 32))


def part_scratch(r):
    return dict(
        ax=((NX, r, 640), BF16), a1=((r, 640), BF16), a2=((r, 640), BF16), slope=((r, 640), F32),
        hs=((NY, r, 160), BF16), hr=((NY, r, 160), BF16),
        ms=((r, 1024), BF16), mz=((7, r, LANES), BF16), m1=((r, LANES), BF16), mf=((NY, r, 1024), BF16),
        gp=((NX, r, 896), BF16), gc=((NX, r, OWN), BF16), g1=((NX, r, OWN), BF16), gx=((3, r, OWN), BF16),
        up=((NX, r, 896), BF16), uc=((NX, r, OWN), BF16), u1=((NX, r, OWN), BF16), ux=((3, r, OWN), BF16),
        gio=((NX, r, OWN), BF16), gir=((NX, r, REST), BF16), uio=((NX, r, OWN), BF16), uir=((NX, r, REST), BF16),
        hdo=((NX, r, OWN), BF16), hdr=((NX, r, REST), BF16),
        bp=((NY, r, 1024), BF16), by=((3, r, 1024), BF16), bs=((r, 1024), BF16),
        bz=((7, r, LANES), BF16), b1=((r, LANES), BF16), bf=((NY, r, 1024), BF16),
        cx=((NX, r, 640), BF16), c1=((r, 640), BF16), c2=((r, 640), BF16), pg=((r, 640), BF16),
        gs=((NY, r, 160), BF16), gr=((NY, r, 160), BF16),
        qs=((r, 640), BF16), qz=((7, r, LANES), BF16), q1=((r, LANES), BF16),
    )


SEMS = 320
OWNERS = 5


class Refs:
    pass


def kernel(*refs):
    patches, grads, wi_in, wo_in, wg_in, wu_in, wd_in = refs[:7]
    s = Refs()
    s.qf, s.ig, s.og, s.gg, s.ug, s.dg = refs[7:13]
    names = iter(refs[13:-3])
    for name in SCRATCH:
        setattr(s, name, next(names))
    halves_of = [Refs() for _ in PARTS]
    for t, (_, r) in zip(halves_of, PARTS):
        for name in part_scratch(r):
            setattr(t, name, next(names))
    send_sems, recv_sems, local_sems = refs[-3:]
    gx, gy, gz = lax.axis_index("gx"), lax.axis_index("gy"), lax.axis_index("gz")
    x, c = gx // 2, gx % 2
    y, z = gy // 2, (gy % 2) * 4 + gz
    ring = (2, 1, 3)
    ring_z = (4, 3, 5, 2, 6, 1, 7)
    to_y = [((y + d) % NY, (gx, ((y + d) % NY) * 2 + z // 4, gz)) for d in ring]
    to_x = [((x + d) % NX, (((x + d) % NX) * 2 + c, gy, gz)) for d in ring]
    to_z = [((z + d) % NZ, (gx, y * 2 + ((z + d) % NZ) // 4, ((z + d) % NZ) % 4)) for d in ring_z]
    to_c = (x * 2 + (1 - c), gy, gz)

    started = []
    count = [0, 0]

    def plan(src, dst, device):
        i = count[0]
        count[0] += 1
        return pltpu.make_async_remote_copy(
            src_ref=src, dst_ref=dst, send_sem=send_sems.at[i], recv_sem=recv_sems.at[i], device_id=device, device_id_type=MESH
        )

    def send(src, dst, device):
        copy = plan(src, dst, device)
        copy.start()
        started.append(copy.wait_send)
        return copy

    def move(src, dst):
        copy = pltpu.make_async_copy(src, dst, local_sems.at[count[1]])
        count[1] += 1
        copy.start()
        return copy

    def arrive(copies):
        for copy in copies:
            copy.wait_recv()

    def cols(i):
        return at(i * LANES, LANES, LANES)

    def scatter_blocks(src, dst, peers, part=slice(None)):
        return [send(src.at[p, :, part], dst.at[k, :, part], device) for k, (p, device) in enumerate(peers)]

    def spread(ref, peers):
        return [send(ref, ref, device) for _, device in peers]

    def scatter_cols(src, dst):
        return [send(src.at[:, cols(p)], dst.at[k], device) for k, (p, device) in enumerate(to_z)]

    def total(own, parts):
        value = own.astype(F32)
        for k in range(parts.shape[0]):
            value = value + parts[k].astype(F32)
        return value

    def in_order(parts):
        return total(parts[0], parts.at[1:])

    def tiles(total_cols, fn):
        full = total_cols // 256

        def step(t, carry):
            fn(pl.multiple_of(t * 256, 256), 256)
            return carry

        lax.fori_loop(0, full, step, 0)
        if total_cols % 256:
            fn(full * 256, total_cols % 256)

    strip = at(y * 160, 160, 16)
    loads = {n: move(r, d) for n, r, d in (
        ("patches", patches, s.p10), ("grads", grads, s.o10),
        ("wi", wi_in, s.wi.at[strip]), ("wo", wo_in, s.wo.at[strip]), ("wd", wd_in, s.wd), ("wg", wg_in, s.wg), ("wu", wu_in, s.wu)
    )}

    barrier = pltpu.get_barrier_semaphore()
    peers = [d for _, d in to_z + to_y + to_x] + [to_c]
    for device in peers:
        pl.semaphore_signal(barrier, inc=1, device_id=device, device_id_type=MESH)

    deal = (lax.broadcasted_iota(jnp.int32, (16, 10), 0) == lax.broadcasted_iota(jnp.int32, (16, 10), 1)).astype(F32).astype(BF16)
    loads["patches"].wait()
    s.pp[...] = dot(deal, s.p10[...]).astype(BF16)
    loads["grads"].wait()
    s.op[...] = dot(deal, s.o10[...]).astype(BF16)
    row = lax.broadcasted_iota(jnp.int32, (ROWS, 128), 0)
    col = lax.broadcasted_iota(jnp.int32, (ROWS, 128), 1)
    pick = jnp.where(col == row + 6 * ((row * 205) >> 11), 1.0, 0.0).astype(BF16)
    pl.semaphore_wait(barrier, len(peers))

    def gather_z(src, buf):
        copies = [send(src, buf.at[at(z * 16, 16, 16)], device) for _, device in to_z]
        buf[at(z * 16, 16, 16), :] = src[...]
        return copies

    p_z = gather_z(s.pp, s.pz)
    loads["wi"].wait()
    wi_y = spread(s.wi.at[strip], to_y)
    arrive(p_z)
    o_z = gather_z(s.op, s.oz)
    loads["wo"].wait()
    wo_y = spread(s.wo.at[strip], to_y[1:])
    s.pf[y] = dot(pick, s.pz[...]).astype(BF16)
    arrive(wi_y)

    mine = at(c * REST, OWN, LANES)
    theirs = at((1 - c) * REST, OWN, LANES)
    give = at(c * LANES, REST, LANES)
    rest = at((1 - c) * OWN, REST, LANES)
    owner = z < OWNERS
    zc = cols(jnp.minimum(z, OWNERS - 1))
    sources = [(z + NZ - d) % NZ < OWNERS for d in ring_z]

    def deal_out(value, src, dst):
        for q in range(NY):
            src[q] = value[:, q * 160 : (q + 1) * 160].astype(BF16)
        dst[y] = src[y]
        return [send(src.at[p], dst.at[y], device) for p, device in to_y]

    def core_sum(whole, other):
        return (whole[:, :, mine].astype(F32) + other[...].astype(F32)).astype(BF16)

    def gather_x(value, buf, other):
        buf[x] = value
        return spread(buf.at[x], to_x), [send(buf.at[x, :, give], other.at[x], to_c)]

    def hand_over(copies, given, buf, other):
        for copy, d in (*zip(copies[1:], ring[1:]), (copies[0], ring[0])):
            arrive([copy])
            p = (x + NX - d) % NX
            given.append(send(buf.at[p, :, give], other.at[p], to_c))

    def flat(ref):
        return ref.reshape(ref.shape[0] * ref.shape[1], ref.shape[2])

    def chain(t, offset, r):
        part = pl.ds(offset, r)
        t.ax[x] = dot_back(s.pf[y, part, :], s.wi[...]).astype(BF16)
        a_x = spread(t.ax.at[x], to_x)
        yield
        arrive(a_x)
        t.a1[...] = in_order(t.ax).astype(BF16)
        a_c = send(t.a1, t.a2, to_c)
        yield
        arrive([a_c])
        gelu_value, gelu_slope = gelu_parts(t.a1[...].astype(F32) + t.a2[...].astype(F32))
        if offset == 0:
            arrive(wo_y)
        t.ms[...] = dot(gelu_value.astype(BF16), s.wo[...]).astype(BF16)
        m_z = scatter_cols(t.ms, t.mz)
        t.slope[...] = gelu_slope
        t.h_y = deal_out(gelu_value, t.hs, t.hr)
        yield
        arrive(m_z)
        t.m1[...] = total(t.ms[:, cols(z)], t.mz).astype(BF16)
        t.mf[y, :, cols(z)] = t.m1[...]
        near, far = (to_z, to_y) if offset == 0 else (to_y, to_z)
        m_near = [send(t.m1, t.mf.at[y, :, cols(z)], device) for _, device in near]
        yield
        arrive(m_near)
        m_far = spread(t.mf.at[y] if offset == 0 else t.mf.at[:, :, cols(z)], far)
        yield
        arrive(m_far)

        def project(weight, out):
            def tile(start, size):
                flat(out)[:, pl.ds(start, size)] = dot(flat(t.mf)[...], weight[:, pl.ds(start, size)]).astype(BF16)

            tiles(896, tile)

        project(s.wg, t.gp)
        g_c = send(t.gp.at[:, :, theirs], t.gc, to_c)
        project(s.wu, t.up)
        u_c = send(t.up.at[:, :, theirs], t.uc, to_c)
        yield
        arrive([g_c])
        t.g1[...] = core_sum(t.gp, t.gc)
        g_x = scatter_blocks(t.g1, t.gx, to_x)
        arrive([u_c])
        t.u1[...] = core_sum(t.up, t.uc)
        u_x = scatter_blocks(t.u1, t.ux, to_x)
        yield
        arrive(g_x)
        arrive(u_x)
        hidden, gate_in, up_in = swiglu_backward(total(t.g1[x], t.gx), total(t.u1[x], t.ux), s.dsum[part, :])
        gi_x, gi_c = gather_x(gate_in, t.gio, t.gir)
        ui_x, ui_c = gather_x(up_in, t.uio, t.uir)
        t.hdo[x] = hidden
        yield
        hand_over(gi_x, gi_c, t.gio, t.gir)
        hand_over(ui_x, ui_c, t.uio, t.uir)
        yield
        arrive(gi_c)
        arrive(ui_c)
        b_y = []
        for k in range(4):
            tile = pl.ds(k * 256, 256)
            flat(t.bp)[:, tile] = (
                dot_back(flat(t.gio)[...], s.wg[tile, mine])
                + dot_back(flat(t.uio)[...], s.wu[tile, mine])
                + dot_back(flat(t.gir)[...], s.wg[tile, rest])
                + dot_back(flat(t.uir)[...], s.wu[tile, rest])
            ).astype(BF16)
            b_y += scatter_blocks(t.bp, t.by, to_y, tile)
        hd_x = spread(t.hdo.at[x], to_x)
        t.hd_c = [send(t.hdo.at[x, :, give], t.hdr.at[x], to_c)]
        yield
        arrive(b_y)
        t.bs[...] = total(t.bp[y], t.by).astype(BF16)
        b_z = scatter_cols(t.bs, t.bz)
        hand_over(hd_x, t.hd_c, t.hdo, t.hdr)
        yield
        arrive(b_z)
        t.b1[...] = (s.of[y, part, cols(z)].astype(F32) + total(t.bs[:, cols(z)], t.bz)).astype(BF16)
        t.bf[y, :, cols(z)] = t.b1[...]
        b_gz = [send(t.b1, t.bf.at[y, :, cols(z)], device) for _, device in to_z]
        yield
        arrive(b_gz)
        t.cx[x] = dot_back(t.bf[y], s.wo[...]).astype(BF16)
        c_x = spread(t.cx.at[x], to_x)
        t.b_gy = spread(t.bf.at[y], to_y)
        yield
        arrive(c_x)
        t.c1[...] = in_order(t.cx).astype(BF16)
        c_c = send(t.c1, t.c2, to_c)
        yield
        arrive([c_c])
        pre_grad = (t.c1[...].astype(F32) + t.c2[...].astype(F32)) * t.slope[...]
        t.pg[...] = pre_grad.astype(BF16)
        t.qs[...] = dot(t.pg[...], s.wi[...]).astype(BF16)
        q_z = [
            (p, plan(t.qs.at[:, cols(jnp.minimum(p, OWNERS - 1))], t.qz.at[k], device)) for k, (p, device) in enumerate(to_z)
        ]
        for p, copy in q_z:
            pl.when(p < OWNERS)(copy.start)
        t.g_y = deal_out(pre_grad, t.gs, t.gr)
        yield
        q_near = [plan(t.q1, s.qf.at[y, part, zc], device) for _, device in near]

        @pl.when(owner)
        def _():
            for _, copy in q_z:
                copy.wait_recv()
            t.q1[...] = total(t.qs[:, zc], t.qz).astype(BF16)
            s.qf[y, part, zc] = t.q1[...]
            for copy in q_near:
                copy.start()

        yield
        if offset == 0:
            for copy, sends in zip(q_near, sources):
                pl.when(sends)(copy.wait_recv)
            q_far = spread(s.qf.at[y, part], far)
        else:
            q_far = [plan(s.qf.at[:, part, zc], s.qf.at[:, part, zc], device) for _, device in far]

            @pl.when(owner)
            def _():
                arrive(q_near)
                for copy in q_far:
                    copy.start()

        yield
        if offset == 0:
            arrive(q_far)
        else:
            for copy, sends in zip(q_far, sources):
                pl.when(sends)(copy.wait_recv)
        for p, copy in q_z:
            pl.when(p < OWNERS)(copy.wait_send)

        @pl.when(owner)
        def _():
            for copy in q_near if offset == 0 else q_near + q_far:
                copy.wait_send()

    def wo_on():
        arrive(o_z)
        s.of[y] = dot(pick, s.oz[...]).astype(BF16)
        halves = [at((y + d) % NY * 160 + h, 80, 16) for d, h in ((3, 0), (1, 80))]
        arrive(wo_y)
        wo_y[:] = [send(s.wo.at[half], s.wo.at[half], device) for half, (_, device) in zip(halves, to_y[1:])]

    def grads_y():
        o_y.extend(spread(s.of.at[y], to_y))
        loads["wd"].wait()

    def down():
        def tile(start, size):
            flat(s.dp)[:, pl.ds(start, size)] = dot_back(flat(s.of)[...], s.wd[pl.ds(start, size), :]).astype(BF16)

        arrive(o_y)
        tiles(896, tile)
        d_c.append(send(s.dp.at[:, :, theirs], s.dc, to_c))
        loads["wg"].wait()
        loads["wu"].wait()

    def down_x():
        arrive(d_c)
        s.d1[...] = core_sum(s.dp, s.dc)
        d_x.extend(scatter_blocks(s.d1, s.dx, to_x))

    def down_sum():
        p_y.extend(spread(s.pf.at[y], to_y))
        arrive(d_x)
        s.dsum[...] = total(s.d1[x], s.dx)

    def by_token(pairs):
        value = 0.0
        for left, right in pairs:
            value = value + dot_tokens(left, right)
        return value.astype(BF16)

    def weight_grad(out, own, other):
        def tile(start, size):
            lefts = [flat(t.mf)[:, pl.ds(start, size)] for t in halves_of]
            out[pl.ds(start, size), mine] = by_token([(a, flat(getattr(t, own))[...]) for a, t in zip(lefts, halves_of)])
            out[pl.ds(start, size), rest] = by_token([(a, flat(getattr(t, other))[...]) for a, t in zip(lefts, halves_of)])

        tiles(1024, tile)

    def down_grad():
        for t in halves_of:
            arrive(t.hd_c)

        def tile(start, size):
            tile_cols = pl.ds(start, size)
            rights = [s.of[:, pl.ds(o, r), tile_cols].reshape(NY * r, size) for o, r in PARTS]
            s.dg[mine, tile_cols] = by_token([(flat(t.hdo)[...], b) for t, b in zip(halves_of, rights)])
            s.dg[rest, tile_cols] = by_token([(flat(t.hdr)[...], b) for t, b in zip(halves_of, rights)])

        tiles(1024, tile)

    def outer_grad():
        for t in halves_of:
            arrive(t.h_y)
            arrive(t.b_gy)
        s.og[...] = by_token([(flat(t.hr)[...], flat(t.bf)[...]) for t in halves_of])

    def inner_grad():
        arrive(p_y)
        for t in halves_of:
            arrive(t.g_y)
        s.ig[...] = by_token([(flat(t.gr)[...], s.pf[:, pl.ds(o, r), :].reshape(NY * r, 640)) for t, (o, r) in zip(halves_of, PARTS)])

    o_y, p_y, d_c, d_x = [], [], [], []
    beside = {
        0: wo_on, 2: grads_y, 4: down, 5: down_x, 6: down_sum,
        9: lambda: weight_grad(s.gg, "gio", "gir"), 10: lambda: weight_grad(s.ug, "uio", "uir"), 11: down_grad,
        14: outer_grad, 15: inner_grad,
    }
    chains = [chain(t, o, r) for t, (o, r) in zip(halves_of, PARTS)]
    for step in range(18):
        for steps in chains:
            next(steps, None)
        if step in beside:
            beside[step]()

    for wait_send in started:
        wait_send()


def local(patches, merge_inner, merge_outer, gate_weight, up_weight, down_weight, out_grad):
    vmem = pl.BlockSpec(memory_space=pltpu.VMEM)
    in_hbm = pl.BlockSpec(memory_space=pltpu.HBM)
    shapes = [(NY, ROWS, 640), (160, 640), (160, 1024), (1024, 896), (1024, 896), (896, 1024)]
    buffers = [*SCRATCH.values(), *(b for _, r in PARTS for b in part_scratch(r).values())]
    arrays = (patches, out_grad, merge_inner.T, merge_outer, gate_weight, up_weight, down_weight)
    results = pl.pallas_call(
        kernel,
        out_shape=[pltpu.VMEM(shape, BF16) for shape in shapes],
        in_specs=[in_hbm] * 7,
        out_specs=[vmem] * 6,
        scratch_shapes=[pltpu.VMEM(shape, dtype) for shape, dtype in buffers]
        + [pltpu.SemaphoreType.DMA((SEMS,)), pltpu.SemaphoreType.DMA((SEMS,)), pltpu.SemaphoreType.DMA((16,))],
        compiler_params=pltpu.CompilerParams(collective_id=0, has_side_effects=True, vmem_limit_bytes=56 * 2**20),
        name="layer",
    )(*(pltpu.with_memory_space_constraint(a, pltpu.HBM) for a in arrays))
    patch_grad, inner_grad, *others = results
    return (patch_grad.reshape(320, 640), inner_grad.T, *others)


def solution(mesh):
    in_specs = (
        P(("gy", "gz"), "gx"),
        P("gx", ("gy", "gz")),
        P(("gy", "gz"), "gx"),
        P("gx", ("gy", "gz")),
        P("gx", ("gy", "gz")),
        P(("gy", "gz"), "gx"),
        P(("gy", "gz"), "gx"),
    )
    out_specs = (
        P(None, "gx"),
        P("gx", ("gy", "gz")),
        P(("gy", "gz"), "gx"),
        P("gx", ("gy", "gz")),
        P("gx", ("gy", "gz")),
        P(("gy", "gz"), "gx"),
    )
    return jax.shard_map(local, mesh=mesh, in_specs=in_specs, out_specs=out_specs, check_vma=False)
```

```python
import jax
import jax.numpy as jnp
from jax import lax
from jax.experimental import pallas as pl
from jax.experimental.pallas import tpu as pltpu
from jax.sharding import PartitionSpec as P

MESH = pl.DeviceIdType.MESH
F32 = jnp.float32
BF16 = jnp.bfloat16
NX, NY, NZ = 4, 4, 8
ROWS = 80
LANES = 128
OWN, REST = 512, 384


def gelu_parts(pre_act):
    normal_cdf = 0.5 * (1.0 + lax.erf(pre_act * 0.7071067811865476))
    normal_pdf = jnp.exp(-0.5 * pre_act * pre_act) * 0.3989422804014327
    return (pre_act * normal_cdf, normal_cdf + pre_act * normal_pdf)


def swiglu_backward(gate_sum, up_sum, down_sum):
    logistic = jax.nn.sigmoid(gate_sum)
    swish_value = gate_sum * logistic
    swish_slope = logistic * (1.0 + gate_sum * (1.0 - logistic))
    hidden = (swish_value * up_sum).astype(BF16)
    gate_in = (down_sum * up_sum * swish_slope).astype(BF16)
    up_in = (down_sum * swish_value).astype(BF16)
    return (hidden, gate_in, up_in)


def dot(left, right):
    return jnp.dot(left, right, preferred_element_type=F32)


def dot_back(left, right):
    return lax.dot_general(left, right, (((1,), (1,)), ((), ())), preferred_element_type=F32)


def dot_tokens(left, right):
    return lax.dot_general(left, right, (((0,), (0,)), ((), ())), preferred_element_type=F32)


def at(start, size, unit):
    return pl.ds(pl.multiple_of(start, unit), size)


SCRATCH = dict(
    wi=((640, 640), BF16), wo=((640, 1024), BF16), wg=((1024, 896), BF16), wu=((1024, 896), BF16), wd=((896, 1024), BF16),
    p10=((10, 640), BF16), o10=((10, 1024), BF16), pp=((16, 640), BF16), op=((16, 1024), BF16),
    pz=((128, 640), BF16), oz=((128, 1024), BF16), pf=((NY, ROWS, 640), BF16), of=((NY, ROWS, 1024), BF16),
    dp=((NX, ROWS, 896), BF16), dc=((NX, ROWS, OWN), BF16), d1=((NX, ROWS, OWN), BF16), dx=((3, ROWS, OWN), BF16),
    dsum=((ROWS, OWN), F32),
)
PARTS = ((0, 48), (48, 32))
Z_FIRST = (0, 48)


def part_scratch(r):
    return dict(
        ax=((NX, r, 640), BF16), a1=((r, 640), BF16), a2=((r, 640), BF16), slope=((r, 640), F32),
        hs=((NY, r, 160), BF16), hr=((NY, r, 160), BF16),
        ms=((r, 1024), BF16), mz=((7, r, LANES), BF16), m1=((r, LANES), BF16), mf=((NY, r, 1024), BF16),
        gp=((NX, r, 896), BF16), gc=((NX, r, OWN), BF16),
        up=((NX, r, 896), BF16), uc=((NX, r, OWN), BF16), gu=((NX, r, 2 * OWN), BF16), gux=((3, r, 2 * OWN), BF16),
        io=((NX, r, 2 * OWN), BF16), gir=((NX, r, REST), BF16), uir=((NX, r, REST), BF16),
        hdo=((NX, r, OWN), BF16), hdr=((NX, r, REST), BF16),
        bp=((NY, r, 1024), BF16), by=((3, r, 1024), BF16), bs=((r, 1024), BF16),
        bz=((7, r, LANES), BF16), b1=((r, LANES), BF16), bf=((NY, r, 1024), BF16),
        cx=((NX, r, 640), BF16), c1=((r, 640), BF16), c2=((r, 640), BF16), pg=((r, 640), BF16),
        gs=((NY, r, 160), BF16), gr=((NY, r, 160), BF16),
        qs=((r, 640), BF16), qz=((7, r, LANES), BF16), q1=((r, LANES), BF16),
    )


SEMS = 320
OWNERS = 5


class Refs:
    pass


def kernel(*refs):
    patches, grads, wi_in, wo_in, wg_in, wu_in, wd_in = refs[:7]
    s = Refs()
    s.qf, s.ig, s.og, s.gg, s.ug, s.dg = refs[7:13]
    names = iter(refs[13:-3])
    for name in SCRATCH:
        setattr(s, name, next(names))
    halves_of = [Refs() for _ in PARTS]
    for t, (_, r) in zip(halves_of, PARTS):
        for name in part_scratch(r):
            setattr(t, name, next(names))
    send_sems, recv_sems, local_sems = refs[-3:]
    gx, gy, gz = lax.axis_index("gx"), lax.axis_index("gy"), lax.axis_index("gz")
    x, c = gx // 2, gx % 2
    y, z = gy // 2, (gy % 2) * 4 + gz
    ring = (2, 1, 3)
    ring_z = (4, 3, 5, 2, 6, 1, 7)
    to_y = [((y + d) % NY, (gx, ((y + d) % NY) * 2 + z // 4, gz)) for d in ring]
    to_x = [((x + d) % NX, (((x + d) % NX) * 2 + c, gy, gz)) for d in ring]
    to_z = [((z + d) % NZ, (gx, y * 2 + ((z + d) % NZ) // 4, ((z + d) % NZ) % 4)) for d in ring_z]
    to_c = (x * 2 + (1 - c), gy, gz)

    started = []
    count = [0, 0]

    def plan(src, dst, device):
        i = count[0]
        count[0] += 1
        return pltpu.make_async_remote_copy(
            src_ref=src, dst_ref=dst, send_sem=send_sems.at[i], recv_sem=recv_sems.at[i], device_id=device, device_id_type=MESH
        )

    def send(src, dst, device):
        copy = plan(src, dst, device)
        copy.start()
        started.append(copy.wait_send)
        return copy

    def move(src, dst):
        copy = pltpu.make_async_copy(src, dst, local_sems.at[count[1]])
        count[1] += 1
        copy.start()
        return copy

    def arrive(copies):
        for copy in copies:
            copy.wait_recv()

    def cols(i):
        return at(i * LANES, LANES, LANES)

    def scatter_blocks(src, dst, peers, part=slice(None)):
        return [send(src.at[p, :, part], dst.at[k, :, part], device) for k, (p, device) in enumerate(peers)]

    def spread(ref, peers):
        return [send(ref, ref, device) for _, device in peers]

    def scatter_cols(src, dst):
        return [send(src.at[:, cols(p)], dst.at[k], device) for k, (p, device) in enumerate(to_z)]

    def total(own, parts):
        value = own.astype(F32)
        for k in range(parts.shape[0]):
            value = value + parts[k].astype(F32)
        return value

    def in_order(parts):
        return total(parts[0], parts.at[1:])

    def tiles(total_cols, fn):
        full = total_cols // 256

        def step(t, carry):
            fn(pl.multiple_of(t * 256, 256), 256)
            return carry

        lax.fori_loop(0, full, step, 0)
        if total_cols % 256:
            fn(full * 256, total_cols % 256)

    strip = at(y * 160, 160, 16)
    loads = {n: move(r, d) for n, r, d in (
        ("patches", patches, s.p10), ("grads", grads, s.o10),
        ("wi", wi_in, s.wi.at[strip]), ("wo", wo_in, s.wo.at[strip]), ("wd", wd_in, s.wd), ("wg", wg_in, s.wg), ("wu", wu_in, s.wu)
    )}

    barrier = pltpu.get_barrier_semaphore()
    peers = [d for _, d in to_z + to_y + to_x] + [to_c]
    for device in peers:
        pl.semaphore_signal(barrier, inc=1, device_id=device, device_id_type=MESH)

    deal = (lax.broadcasted_iota(jnp.int32, (16, 10), 0) == lax.broadcasted_iota(jnp.int32, (16, 10), 1)).astype(F32).astype(BF16)
    loads["patches"].wait()
    s.pp[...] = dot(deal, s.p10[...]).astype(BF16)
    loads["grads"].wait()
    s.op[...] = dot(deal, s.o10[...]).astype(BF16)
    row = lax.broadcasted_iota(jnp.int32, (ROWS, 128), 0)
    col = lax.broadcasted_iota(jnp.int32, (ROWS, 128), 1)
    pick = jnp.where(col == row + 6 * ((row * 205) >> 11), 1.0, 0.0).astype(BF16)
    pl.semaphore_wait(barrier, len(peers))

    def gather_z(src, buf):
        copies = [send(src, buf.at[at(z * 16, 16, 16)], device) for _, device in to_z]
        buf[at(z * 16, 16, 16), :] = src[...]
        return copies

    p_z = gather_z(s.pp, s.pz)
    loads["wi"].wait()
    wi_y = spread(s.wi.at[strip], to_y[1:])
    arrive(p_z)
    s.pf[y] = dot(pick, s.pz[...]).astype(BF16)

    def pass_on(buf, copies):
        halves = [at((y + d) % NY * 160 + h, 80, 16) for d, h in ((3, 0), (1, 80))]
        arrive(copies)
        return [send(buf.at[half], buf.at[half], device) for half, (_, device) in zip(halves, to_y[1:])]

    wi_y = pass_on(s.wi, wi_y)
    o_z = gather_z(s.op, s.oz)
    loads["wo"].wait()
    wo_y = spread(s.wo.at[strip], to_y[1:])
    arrive(wi_y)

    mine = at(c * REST, OWN, LANES)
    theirs = at((1 - c) * REST, OWN, LANES)
    give = at(c * LANES, REST, LANES)
    rest = at((1 - c) * OWN, REST, LANES)
    owner = z < OWNERS
    zc = cols(jnp.minimum(z, OWNERS - 1))
    sources = [(z + NZ - d) % NZ < OWNERS for d in ring_z]

    def deal_out(value, src, dst):
        for q in range(NY):
            src[q] = value[:, q * 160 : (q + 1) * 160].astype(BF16)
        dst[y] = src[y]
        return [send(src.at[p], dst.at[y], device) for p, device in to_y]

    def core_sum(whole, other):
        return (whole[:, :, mine].astype(F32) + other[...].astype(F32)).astype(BF16)

    def flat(ref):
        return ref.reshape(ref.shape[0] * ref.shape[1], ref.shape[2])

    def chain(t, offset, r):
        part = pl.ds(offset, r)
        z_first = offset in Z_FIRST
        t.ax[x] = dot_back(s.pf[y, part, :], s.wi[...]).astype(BF16)
        a_x = spread(t.ax.at[x], to_x)
        yield
        arrive(a_x)
        t.a1[...] = in_order(t.ax).astype(BF16)
        a_c = send(t.a1, t.a2, to_c)
        yield
        arrive([a_c])
        gelu_value, gelu_slope = gelu_parts(t.a1[...].astype(F32) + t.a2[...].astype(F32))
        if offset == 0:
            arrive(wo_y)
        t.ms[...] = dot(gelu_value.astype(BF16), s.wo[...]).astype(BF16)
        m_z = scatter_cols(t.ms, t.mz)
        t.slope[...] = gelu_slope
        t.h_y = deal_out(gelu_value, t.hs, t.hr)
        yield
        arrive(m_z)
        t.m1[...] = total(t.ms[:, cols(z)], t.mz).astype(BF16)
        t.mf[y, :, cols(z)] = t.m1[...]
        near, far = (to_z, to_y) if z_first else (to_y, to_z)
        m_near = [send(t.m1, t.mf.at[y, :, cols(z)], device) for _, device in near]
        yield
        arrive(m_near)
        m_far = spread(t.mf.at[y] if z_first else t.mf.at[:, :, cols(z)], far)
        yield
        arrive(m_far)

        def project(weight, out):
            def tile(start, size):
                flat(out)[:, pl.ds(start, size)] = dot(flat(t.mf)[...], weight[:, pl.ds(start, size)]).astype(BF16)

            tiles(896, tile)

        project(s.wg, t.gp)
        g_c = send(t.gp.at[:, :, theirs], t.gc, to_c)
        project(s.wu, t.up)
        u_c = send(t.up.at[:, :, theirs], t.uc, to_c)
        yield
        arrive([g_c])
        t.gu[:, :, :OWN] = core_sum(t.gp, t.gc)
        arrive([u_c])
        t.gu[:, :, OWN:] = core_sum(t.up, t.uc)
        gu_x = scatter_blocks(t.gu, t.gux, to_x)
        yield
        arrive(gu_x)
        sums = total(t.gu[x], t.gux)
        hidden, gate_in, up_in = swiglu_backward(sums[:, :OWN], sums[:, OWN:], s.dsum[part, :])
        t.io[x, :, :OWN] = gate_in
        t.io[x, :, OWN:] = up_in
        io_x = spread(t.io.at[x], to_x)
        t.hdo[x] = hidden
        yield
        arrive(io_x)
        gi_c = [send(t.io.at[:, :, give], t.gir, to_c)]
        ui_c = [send(t.io.at[:, :, at(OWN + c * LANES, REST, LANES)], t.uir, to_c)]
        yield
        arrive(gi_c)
        arrive(ui_c)
        b_y = []
        for k in range(4):
            tile = pl.ds(k * 256, 256)
            flat(t.bp)[:, tile] = (
                dot_back(flat(t.io)[:, :OWN], s.wg[tile, mine])
                + dot_back(flat(t.io)[:, OWN:], s.wu[tile, mine])
                + dot_back(flat(t.gir)[...], s.wg[tile, rest])
                + dot_back(flat(t.uir)[...], s.wu[tile, rest])
            ).astype(BF16)
            b_y += scatter_blocks(t.bp, t.by, to_y, tile)
        hd_x = spread(t.hdo.at[x], to_x)
        yield
        arrive(b_y)
        t.bs[...] = total(t.bp[y], t.by).astype(BF16)
        b_z = scatter_cols(t.bs, t.bz)
        arrive(hd_x)
        t.hd_c = [send(t.hdo.at[:, :, give], t.hdr, to_c)]
        yield
        arrive(b_z)
        t.b1[...] = (s.of[y, part, cols(z)].astype(F32) + total(t.bs[:, cols(z)], t.bz)).astype(BF16)
        t.bf[y, :, cols(z)] = t.b1[...]
        b_gz = [send(t.b1, t.bf.at[y, :, cols(z)], device) for _, device in to_z]
        yield
        arrive(b_gz)
        t.cx[x] = dot_back(t.bf[y], s.wo[...]).astype(BF16)
        c_x = spread(t.cx.at[x], to_x)
        t.b_gy = spread(t.bf.at[y], to_y)
        yield
        arrive(c_x)
        t.c1[...] = in_order(t.cx).astype(BF16)
        c_c = send(t.c1, t.c2, to_c)
        yield
        arrive([c_c])
        pre_grad = (t.c1[...].astype(F32) + t.c2[...].astype(F32)) * t.slope[...]
        t.pg[...] = pre_grad.astype(BF16)
        t.qs[...] = dot(t.pg[...], s.wi[...]).astype(BF16)
        q_z = [
            (p, plan(t.qs.at[:, cols(jnp.minimum(p, OWNERS - 1))], t.qz.at[k], device)) for k, (p, device) in enumerate(to_z)
        ]
        for p, copy in q_z:
            pl.when(p < OWNERS)(copy.start)
        t.g_y = deal_out(pre_grad, t.gs, t.gr)
        yield
        q_near = [plan(t.q1, s.qf.at[y, part, zc], device) for _, device in near]

        @pl.when(owner)
        def _():
            for _, copy in q_z:
                copy.wait_recv()
            t.q1[...] = total(t.qs[:, zc], t.qz).astype(BF16)
            s.qf[y, part, zc] = t.q1[...]
            for copy in q_near:
                copy.start()

        yield
        if z_first:
            for copy, sends in zip(q_near, sources):
                pl.when(sends)(copy.wait_recv)
            q_far = spread(s.qf.at[y, part], far)
        else:
            q_far = [plan(s.qf.at[:, part, zc], s.qf.at[:, part, zc], device) for _, device in far]

            @pl.when(owner)
            def _():
                arrive(q_near)
                for copy in q_far:
                    copy.start()

        yield
        if z_first:
            arrive(q_far)
        else:
            for copy, sends in zip(q_far, sources):
                pl.when(sends)(copy.wait_recv)
        for p, copy in q_z:
            pl.when(p < OWNERS)(copy.wait_send)

        @pl.when(owner)
        def _():
            for copy in q_near if z_first else q_near + q_far:
                copy.wait_send()

    def wo_on():
        arrive(o_z)
        s.of[y] = dot(pick, s.oz[...]).astype(BF16)
        wo_y[:] = pass_on(s.wo, wo_y)

    def grads_y():
        o_y.extend(spread(s.of.at[y], to_y))
        loads["wd"].wait()

    def down():
        def tile(start, size):
            flat(s.dp)[:, pl.ds(start, size)] = dot_back(flat(s.of)[...], s.wd[pl.ds(start, size), :]).astype(BF16)

        arrive(o_y)
        tiles(896, tile)
        d_c.append(send(s.dp.at[:, :, theirs], s.dc, to_c))
        loads["wg"].wait()
        loads["wu"].wait()

    def down_x():
        arrive(d_c)
        s.d1[...] = core_sum(s.dp, s.dc)
        d_x.extend(scatter_blocks(s.d1, s.dx, to_x))

    def down_sum():
        p_y.extend(spread(s.pf.at[y], to_y))
        arrive(d_x)
        s.dsum[...] = total(s.d1[x], s.dx)

    def by_token(pairs):
        value = 0.0
        for left, right in pairs:
            value = value + dot_tokens(left, right)
        return value.astype(BF16)

    def weight_grad(out, own, other):
        def tile(start, size):
            lefts = [flat(t.mf)[:, pl.ds(start, size)] for t in halves_of]
            out[pl.ds(start, size), mine] = by_token([(a, flat(t.io)[:, own]) for a, t in zip(lefts, halves_of)])
            out[pl.ds(start, size), rest] = by_token([(a, flat(getattr(t, other))[...]) for a, t in zip(lefts, halves_of)])

        tiles(1024, tile)

    def down_grad():
        for t in halves_of:
            arrive(t.hd_c)

        def tile(start, size):
            tile_cols = pl.ds(start, size)
            rights = [s.of[:, pl.ds(o, r), tile_cols].reshape(NY * r, size) for o, r in PARTS]
            s.dg[mine, tile_cols] = by_token([(flat(t.hdo)[...], b) for t, b in zip(halves_of, rights)])
            s.dg[rest, tile_cols] = by_token([(flat(t.hdr)[...], b) for t, b in zip(halves_of, rights)])

        tiles(1024, tile)

    def outer_grad():
        for t in halves_of:
            arrive(t.h_y)
            arrive(t.b_gy)
        s.og[...] = by_token([(flat(t.hr)[...], flat(t.bf)[...]) for t in halves_of])

    def inner_grad():
        arrive(p_y)
        for t in halves_of:
            arrive(t.g_y)
        s.ig[...] = by_token([(flat(t.gr)[...], s.pf[:, pl.ds(o, r), :].reshape(NY * r, 640)) for t, (o, r) in zip(halves_of, PARTS)])

    o_y, p_y, d_c, d_x = [], [], [], []
    sent = []
    beside = {
        0: wo_on, 2: grads_y, 4: down, 5: down_x, 6: down_sum,
        9: lambda: weight_grad(s.gg, pl.ds(0, OWN), "gir"), 10: lambda: weight_grad(s.ug, pl.ds(OWN, OWN), "uir"), 11: down_grad,
        14: outer_grad, 15: inner_grad,
    }
    chains = [chain(t, o, r) for t, (o, r) in zip(halves_of, PARTS)]
    for step in range(18):
        for steps in chains:
            next(steps, None)
        if step in beside:
            beside[step]()
        sent.append(list(started))
        started.clear()
        if step >= 3:
            for wait_send in sent[step - 3]:
                wait_send()

    for wait_send in sum(sent[-3:], []):
        wait_send()


def local(patches, merge_inner, merge_outer, gate_weight, up_weight, down_weight, out_grad):
    vmem = pl.BlockSpec(memory_space=pltpu.VMEM)
    in_hbm = pl.BlockSpec(memory_space=pltpu.HBM)
    shapes = [(NY, ROWS, 640), (160, 640), (160, 1024), (1024, 896), (1024, 896), (896, 1024)]
    buffers = [*SCRATCH.values(), *(b for _, r in PARTS for b in part_scratch(r).values())]
    arrays = (patches, out_grad, merge_inner.T, merge_outer, gate_weight, up_weight, down_weight)
    results = pl.pallas_call(
        kernel,
        out_shape=[pltpu.VMEM(shape, BF16) for shape in shapes],
        in_specs=[in_hbm] * 7,
        out_specs=[vmem] * 6,
        scratch_shapes=[pltpu.VMEM(shape, dtype) for shape, dtype in buffers]
        + [pltpu.SemaphoreType.DMA((SEMS,)), pltpu.SemaphoreType.DMA((SEMS,)), pltpu.SemaphoreType.DMA((16,))],
        compiler_params=pltpu.CompilerParams(collective_id=0, has_side_effects=True, vmem_limit_bytes=56 * 2**20),
        name="layer",
    )(*(pltpu.with_memory_space_constraint(a, pltpu.HBM) for a in arrays))
    patch_grad, inner_grad, *others = results
    return (patch_grad.reshape(320, 640), inner_grad.T, *others)


def solution(mesh):
    in_specs = (
        P(("gy", "gz"), "gx"),
        P("gx", ("gy", "gz")),
        P(("gy", "gz"), "gx"),
        P("gx", ("gy", "gz")),
        P("gx", ("gy", "gz")),
        P(("gy", "gz"), "gx"),
        P(("gy", "gz"), "gx"),
    )
    out_specs = (
        P(None, "gx"),
        P("gx", ("gy", "gz")),
        P(("gy", "gz"), "gx"),
        P("gx", ("gy", "gz")),
        P("gx", ("gy", "gz")),
        P(("gy", "gz"), "gx"),
    )
    return jax.shard_map(local, mesh=mesh, in_specs=in_specs, out_specs=out_specs, check_vma=False)
```

```python
import jax
import jax.numpy as jnp
from jax import lax
from jax.experimental import pallas as pl
from jax.experimental.pallas import tpu as pltpu
from jax.sharding import PartitionSpec as P

MESH = pl.DeviceIdType.MESH
F32 = jnp.float32
BF16 = jnp.bfloat16
NX, NY, NZ = 4, 4, 8
ROWS = 80
LANES = 128
OWN, REST = 512, 384


def gelu_parts(pre_act):
    normal_cdf = 0.5 * (1.0 + lax.erf(pre_act * 0.7071067811865476))
    normal_pdf = jnp.exp(-0.5 * pre_act * pre_act) * 0.3989422804014327
    return (pre_act * normal_cdf, normal_cdf + pre_act * normal_pdf)


def swiglu_backward(gate_sum, up_sum, down_sum):
    logistic = jax.nn.sigmoid(gate_sum)
    swish_value = gate_sum * logistic
    swish_slope = logistic * (1.0 + gate_sum * (1.0 - logistic))
    hidden = (swish_value * up_sum).astype(BF16)
    gate_in = (down_sum * up_sum * swish_slope).astype(BF16)
    up_in = (down_sum * swish_value).astype(BF16)
    return (hidden, gate_in, up_in)


def dot(left, right):
    return jnp.dot(left, right, preferred_element_type=F32)


def dot_back(left, right):
    return lax.dot_general(left, right, (((1,), (1,)), ((), ())), preferred_element_type=F32)


def dot_tokens(left, right):
    return lax.dot_general(left, right, (((0,), (0,)), ((), ())), preferred_element_type=F32)


def at(start, size, unit):
    return pl.ds(pl.multiple_of(start, unit), size)


SCRATCH = dict(
    wi=((640, 640), BF16), wo=((640, 1024), BF16), wot=((1024, 640), BF16), wg=((1024, 896), BF16), wu=((1024, 896), BF16), wd=((896, 1024), BF16),
    p10=((10, 640), BF16), o10=((10, 1024), BF16), pp=((16, 640), BF16), op=((16, 1024), BF16),
    pz=((128, 640), BF16), oz=((128, 1024), BF16), pf=((NY, ROWS, 640), BF16), of=((NY, ROWS, 1024), BF16),
    dp=((NX, ROWS, 896), BF16), dc=((NX, ROWS, OWN), BF16), d1=((NX, ROWS, OWN), BF16), dx=((3, ROWS, OWN), BF16),
    dsum=((ROWS, OWN), F32),
)
PARTS = ((0, 48), (48, 32))
Z_FIRST = (0, 48)


def part_scratch(r):
    return dict(
        ax=((NX, r, 640), BF16), a1=((r, 640), BF16), a2=((r, 640), BF16), slope=((r, 640), F32),
        hs=((NY, r, 160), BF16), hr=((NY, r, 160), BF16),
        ms=((r, 1024), BF16), mz=((7, r, LANES), BF16), m1=((r, LANES), BF16), mf=((NY, r, 1024), BF16),
        gp=((NX, r, 896), BF16), gc=((NX, r, OWN), BF16),
        up=((NX, r, 896), BF16), uc=((NX, r, OWN), BF16), gu=((NX, r, 2 * OWN), BF16), gux=((3, r, 2 * OWN), BF16),
        io=((NX, r, 2 * OWN), BF16), gir=((NX, r, REST), BF16), uir=((NX, r, REST), BF16),
        hdo=((NX, r, OWN), BF16), hdr=((NX, r, REST), BF16),
        bp=((NY, r, 1024), BF16), by=((3, r, 1024), BF16), bs=((r, 1024), BF16),
        bz=((7, r, LANES), BF16), b1=((r, LANES), BF16), bf=((NY, r, 1024), BF16),
        cx=((NX, r, 640), BF16), c1=((r, 640), BF16), c2=((r, 640), BF16), pg=((r, 640), BF16),
        gs=((NY, r, 160), BF16), gr=((NY, r, 160), BF16),
        qs=((r, 640), BF16), qz=((7, r, LANES), BF16), q1=((r, LANES), BF16),
    )


SEMS = 320
OWNERS = 5


class Refs:
    pass


def kernel(*refs):
    patches, grads, wi_in, wo_in, wg_in, wu_in, wd_in = refs[:7]
    s = Refs()
    s.qf, s.ig, s.og, s.gg, s.ug, s.dg = refs[7:13]
    names = iter(refs[13:-3])
    for name in SCRATCH:
        setattr(s, name, next(names))
    halves_of = [Refs() for _ in PARTS]
    for t, (_, r) in zip(halves_of, PARTS):
        for name in part_scratch(r):
            setattr(t, name, next(names))
    send_sems, recv_sems, local_sems = refs[-3:]
    gx, gy, gz = lax.axis_index("gx"), lax.axis_index("gy"), lax.axis_index("gz")
    x, c = gx // 2, gx % 2
    y, z = gy // 2, (gy % 2) * 4 + gz
    ring = (2, 1, 3)
    ring_z = (4, 5, 3, 6, 2, 7, 1)
    to_y = [((y + d) % NY, (gx, ((y + d) % NY) * 2 + z // 4, gz)) for d in ring]
    to_x = [((x + d) % NX, (((x + d) % NX) * 2 + c, gy, gz)) for d in ring]
    to_z = [((z + d) % NZ, (gx, y * 2 + ((z + d) % NZ) // 4, ((z + d) % NZ) % 4)) for d in ring_z]
    to_c = (x * 2 + (1 - c), gy, gz)

    started = []
    count = [0, 0]

    def plan(src, dst, device):
        i = count[0]
        count[0] += 1
        return pltpu.make_async_remote_copy(
            src_ref=src, dst_ref=dst, send_sem=send_sems.at[i], recv_sem=recv_sems.at[i], device_id=device, device_id_type=MESH
        )

    def send(src, dst, device):
        copy = plan(src, dst, device)
        copy.start()
        started.append(copy.wait_send)
        return copy

    def move(src, dst):
        copy = pltpu.make_async_copy(src, dst, local_sems.at[count[1]])
        count[1] += 1
        copy.start()
        return copy

    def arrive(copies):
        for copy in copies:
            copy.wait_recv()

    def cols(i):
        return at(i * LANES, LANES, LANES)

    def scatter_blocks(src, dst, peers, part=slice(None)):
        return [send(src.at[p, :, part], dst.at[k, :, part], device) for k, (p, device) in enumerate(peers)]

    def spread(ref, peers):
        return [send(ref, ref, device) for _, device in peers]

    def scatter_cols(src, dst):
        return [send(src.at[:, cols(p)], dst.at[k], device) for k, (p, device) in enumerate(to_z)]

    def total(own, parts):
        value = own.astype(F32)
        for k in range(parts.shape[0]):
            value = value + parts[k].astype(F32)
        return value

    def in_order(parts):
        return total(parts[0], parts.at[1:])

    def tiles(total_cols, fn):
        full = total_cols // 256

        def step(t, carry):
            fn(pl.multiple_of(t * 256, 256), 256)
            return carry

        lax.fori_loop(0, full, step, 0)
        if total_cols % 256:
            fn(full * 256, total_cols % 256)

    strip = at(y * 160, 160, 16)
    loads = {n: move(r, d) for n, r, d in (
        ("patches", patches, s.p10), ("grads", grads, s.o10),
        ("wi", wi_in, s.wi.at[strip]), ("wo", wo_in, s.wo.at[strip]), ("wd", wd_in, s.wd), ("wg", wg_in, s.wg), ("wu", wu_in, s.wu)
    )}

    barrier = pltpu.get_barrier_semaphore()
    peers = [d for _, d in to_z + to_y + to_x] + [to_c]
    for device in peers:
        pl.semaphore_signal(barrier, inc=1, device_id=device, device_id_type=MESH)

    deal = (lax.broadcasted_iota(jnp.int32, (16, 10), 0) == lax.broadcasted_iota(jnp.int32, (16, 10), 1)).astype(F32).astype(BF16)
    loads["patches"].wait()
    s.pp[...] = dot(deal, s.p10[...]).astype(BF16)
    loads["grads"].wait()
    s.op[...] = dot(deal, s.o10[...]).astype(BF16)
    row = lax.broadcasted_iota(jnp.int32, (ROWS, 128), 0)
    col = lax.broadcasted_iota(jnp.int32, (ROWS, 128), 1)
    pick = jnp.where(col == row + 6 * ((row * 205) >> 11), 1.0, 0.0).astype(BF16)
    pl.semaphore_wait(barrier, len(peers))

    def gather_z(src, buf):
        copies = [send(src, buf.at[at(z * 16, 16, 16)], device) for _, device in to_z]
        buf[at(z * 16, 16, 16), :] = src[...]
        return copies

    p_z = gather_z(s.pp, s.pz)
    loads["wi"].wait()
    wi_y = spread(s.wi.at[strip], to_y[1:])
    arrive(p_z)
    s.pf[y] = dot(pick, s.pz[...]).astype(BF16)

    def pass_on(buf, copies):
        halves = [at((y + d) % NY * 160 + h, 80, 16) for d, h in ((3, 0), (1, 80))]
        arrive(copies)
        return [send(buf.at[half], buf.at[half], device) for half, (_, device) in zip(halves, to_y[1:])]

    wi_y = pass_on(s.wi, wi_y)
    o_z = gather_z(s.op, s.oz)
    loads["wo"].wait()
    wo_y = spread(s.wo.at[strip], to_y[1:])
    arrive(wi_y)

    mine = at(c * REST, OWN, LANES)
    theirs = at((1 - c) * REST, OWN, LANES)
    give = at(c * LANES, REST, LANES)
    rest = at((1 - c) * OWN, REST, LANES)
    owner = z < OWNERS
    zc = cols(jnp.minimum(z, OWNERS - 1))
    sources = [(z + NZ - d) % NZ < OWNERS for d in ring_z]

    def deal_out(value, src, dst):
        for q in range(NY):
            src[q] = value[:, q * 160 : (q + 1) * 160].astype(BF16)
        dst[y] = src[y]
        return [send(src.at[p], dst.at[y], device) for p, device in to_y]

    def core_sum(whole, other):
        return (whole[:, :, mine].astype(F32) + other[...].astype(F32)).astype(BF16)

    def flat(ref):
        return ref.reshape(ref.shape[0] * ref.shape[1], ref.shape[2])

    def chain(t, offset, r):
        part = pl.ds(offset, r)
        z_first = offset in Z_FIRST
        t.ax[x] = dot_back(s.pf[y, part, :], s.wi[...]).astype(BF16)
        a_x = spread(t.ax.at[x], to_x)
        yield
        arrive(a_x)
        t.a1[...] = in_order(t.ax).astype(BF16)
        a_c = send(t.a1, t.a2, to_c)
        yield
        arrive([a_c])
        gelu_value, gelu_slope = gelu_parts(t.a1[...].astype(F32) + t.a2[...].astype(F32))
        if offset == 0:
            arrive(wo_y)
        t.ms[...] = dot(gelu_value.astype(BF16), s.wo[...]).astype(BF16)
        m_z = scatter_cols(t.ms, t.mz)
        t.slope[...] = gelu_slope
        t.h_y = deal_out(gelu_value, t.hs, t.hr)
        yield
        arrive(m_z)
        t.m1[...] = total(t.ms[:, cols(z)], t.mz).astype(BF16)
        t.mf[y, :, cols(z)] = t.m1[...]
        near, far = (to_z, to_y) if z_first else (to_y, to_z)
        m_near = [send(t.m1, t.mf.at[y, :, cols(z)], device) for _, device in near]
        yield
        arrive(m_near)
        m_far = spread(t.mf.at[y] if z_first else t.mf.at[:, :, cols(z)], far)
        yield
        arrive(m_far)

        def project(weight, out):
            def tile(start, size):
                flat(out)[:, pl.ds(start, size)] = dot(flat(t.mf)[...], weight[:, pl.ds(start, size)]).astype(BF16)

            tiles(896, tile)

        project(s.wg, t.gp)
        g_c = send(t.gp.at[:, :, theirs], t.gc, to_c)
        project(s.wu, t.up)
        u_c = send(t.up.at[:, :, theirs], t.uc, to_c)
        yield
        arrive([g_c])
        t.gu[:, :, :OWN] = core_sum(t.gp, t.gc)
        arrive([u_c])
        t.gu[:, :, OWN:] = core_sum(t.up, t.uc)
        gu_x = scatter_blocks(t.gu, t.gux, to_x)
        yield
        arrive(gu_x)
        sums = total(t.gu[x], t.gux)
        hidden, gate_in, up_in = swiglu_backward(sums[:, :OWN], sums[:, OWN:], s.dsum[part, :])
        t.io[x, :, :OWN] = gate_in
        t.io[x, :, OWN:] = up_in
        io_x = spread(t.io.at[x], to_x)
        t.hdo[x] = hidden
        yield
        arrive(io_x)
        gi_c = [send(t.io.at[:, :, give], t.gir, to_c)]
        ui_c = [send(t.io.at[:, :, at(OWN + c * LANES, REST, LANES)], t.uir, to_c)]
        yield
        arrive(gi_c)
        arrive(ui_c)
        b_y = []
        for k in range(4):
            tile = pl.ds(k * 256, 256)
            flat(t.bp)[:, tile] = (
                dot_back(flat(t.io)[:, :OWN], s.wg[tile, mine])
                + dot_back(flat(t.io)[:, OWN:], s.wu[tile, mine])
                + dot_back(flat(t.gir)[...], s.wg[tile, rest])
                + dot_back(flat(t.uir)[...], s.wu[tile, rest])
            ).astype(BF16)
            b_y += scatter_blocks(t.bp, t.by, to_y, tile)
        hd_x = spread(t.hdo.at[x], to_x)
        yield
        arrive(b_y)
        t.bs[...] = total(t.bp[y], t.by).astype(BF16)
        b_z = scatter_cols(t.bs, t.bz)
        arrive(hd_x)
        t.hd_c = [send(t.hdo.at[:, :, give], t.hdr, to_c)]
        yield
        arrive(b_z)
        t.b1[...] = (s.of[y, part, cols(z)].astype(F32) + total(t.bs[:, cols(z)], t.bz)).astype(BF16)
        t.bf[y, :, cols(z)] = t.b1[...]
        b_gz = [send(t.b1, t.bf.at[y, :, cols(z)], device) for _, device in to_z]
        yield
        arrive(b_gz)
        t.cx[x] = dot(t.bf[y], s.wot[...]).astype(BF16)
        c_x = spread(t.cx.at[x], to_x)
        t.b_gy = spread(t.bf.at[y], to_y)
        yield
        arrive(c_x)
        t.c1[...] = in_order(t.cx).astype(BF16)
        c_c = send(t.c1, t.c2, to_c)
        yield
        arrive([c_c])
        pre_grad = (t.c1[...].astype(F32) + t.c2[...].astype(F32)) * t.slope[...]
        t.pg[...] = pre_grad.astype(BF16)
        t.qs[...] = dot(t.pg[...], s.wi[...]).astype(BF16)
        q_z = [
            (p, plan(t.qs.at[:, cols(jnp.minimum(p, OWNERS - 1))], t.qz.at[k], device)) for k, (p, device) in enumerate(to_z)
        ]
        for p, copy in q_z:
            pl.when(p < OWNERS)(copy.start)
        t.g_y = deal_out(pre_grad, t.gs, t.gr)
        yield
        q_near = [plan(t.q1, s.qf.at[y, part, zc], device) for _, device in near]

        @pl.when(owner)
        def _():
            for _, copy in q_z:
                copy.wait_recv()
            t.q1[...] = total(t.qs[:, zc], t.qz).astype(BF16)
            s.qf[y, part, zc] = t.q1[...]
            for copy in q_near:
                copy.start()

        yield
        if z_first:
            for copy, sends in zip(q_near, sources):
                pl.when(sends)(copy.wait_recv)
            q_far = spread(s.qf.at[y, part], far)
        else:
            q_far = [plan(s.qf.at[:, part, zc], s.qf.at[:, part, zc], device) for _, device in far]

            @pl.when(owner)
            def _():
                arrive(q_near)
                for copy in q_far:
                    copy.start()

        yield
        if z_first:
            arrive(q_far)
        else:
            for copy, sends in zip(q_far, sources):
                pl.when(sends)(copy.wait_recv)
        for p, copy in q_z:
            pl.when(p < OWNERS)(copy.wait_send)

        @pl.when(owner)
        def _():
            for copy in q_near if z_first else q_near + q_far:
                copy.wait_send()

    def wo_on():
        arrive(o_z)
        s.of[y] = dot(pick, s.oz[...]).astype(BF16)
        wo_y[:] = pass_on(s.wo, wo_y)

    def grads_y():
        o_y.extend(spread(s.of.at[y], to_y))
        loads["wd"].wait()

    def down():
        def tile(start, size):
            flat(s.dp)[:, pl.ds(start, size)] = dot_back(flat(s.of)[...], s.wd[pl.ds(start, size), :]).astype(BF16)

        arrive(o_y)
        tiles(896, tile)
        d_c.append(send(s.dp.at[:, :, theirs], s.dc, to_c))
        loads["wg"].wait()
        loads["wu"].wait()

    def down_x():
        arrive(d_c)
        s.d1[...] = core_sum(s.dp, s.dc)
        d_x.extend(scatter_blocks(s.d1, s.dx, to_x))

    def down_sum():
        p_y.extend(spread(s.pf.at[y], to_y))
        arrive(d_x)
        s.dsum[...] = total(s.d1[x], s.dx)

    def turn_outer():
        s.wot[...] = s.wo[...].T

    def by_token(pairs):
        value = 0.0
        for left, right in pairs:
            value = value + dot_tokens(left, right)
        return value.astype(BF16)

    def weight_grad(out, own, other):
        def tile(start, size):
            lefts = [flat(t.mf)[:, pl.ds(start, size)] for t in halves_of]
            out[pl.ds(start, size), mine] = by_token([(a, flat(t.io)[:, own]) for a, t in zip(lefts, halves_of)])
            out[pl.ds(start, size), rest] = by_token([(a, flat(getattr(t, other))[...]) for a, t in zip(lefts, halves_of)])

        tiles(1024, tile)

    def down_grad():
        for t in halves_of:
            arrive(t.hd_c)

        def tile(start, size):
            tile_cols = pl.ds(start, size)
            rights = [s.of[:, pl.ds(o, r), tile_cols].reshape(NY * r, size) for o, r in PARTS]
            s.dg[mine, tile_cols] = by_token([(flat(t.hdo)[...], b) for t, b in zip(halves_of, rights)])
            s.dg[rest, tile_cols] = by_token([(flat(t.hdr)[...], b) for t, b in zip(halves_of, rights)])

        tiles(1024, tile)

    def outer_grad():
        for t in halves_of:
            arrive(t.h_y)
            arrive(t.b_gy)
        s.og[...] = by_token([(flat(t.hr)[...], flat(t.bf)[...]) for t in halves_of])

    def inner_grad():
        arrive(p_y)
        for t in halves_of:
            arrive(t.g_y)
        s.ig[...] = by_token([(flat(t.gr)[...], s.pf[:, pl.ds(o, r), :].reshape(NY * r, 640)) for t, (o, r) in zip(halves_of, PARTS)])

    o_y, p_y, d_c, d_x = [], [], [], []
    sent = []
    beside = {
        0: wo_on, 2: grads_y, 4: down, 5: down_x, 6: down_sum, 7: turn_outer,
        9: lambda: weight_grad(s.gg, pl.ds(0, OWN), "gir"), 10: lambda: weight_grad(s.ug, pl.ds(OWN, OWN), "uir"), 11: down_grad,
        14: outer_grad, 15: inner_grad,
    }
    chains = [chain(t, o, r) for t, (o, r) in zip(halves_of, PARTS)]
    for step in range(18):
        for steps in chains:
            next(steps, None)
        if step in beside:
            beside[step]()
        sent.append(list(started))
        started.clear()
        if step >= 3:
            for wait_send in sent[step - 3]:
                wait_send()

    for wait_send in sum(sent[-3:], []):
        wait_send()


def local(patches, merge_inner, merge_outer, gate_weight, up_weight, down_weight, out_grad):
    vmem = pl.BlockSpec(memory_space=pltpu.VMEM)
    in_hbm = pl.BlockSpec(memory_space=pltpu.HBM)
    shapes = [(NY, ROWS, 640), (160, 640), (160, 1024), (1024, 896), (1024, 896), (896, 1024)]
    buffers = [*SCRATCH.values(), *(b for _, r in PARTS for b in part_scratch(r).values())]
    arrays = (patches, out_grad, merge_inner.T, merge_outer, gate_weight, up_weight, down_weight)
    results = pl.pallas_call(
        kernel,
        out_shape=[pltpu.VMEM(shape, BF16) for shape in shapes],
        in_specs=[in_hbm] * 7,
        out_specs=[vmem] * 6,
        scratch_shapes=[pltpu.VMEM(shape, dtype) for shape, dtype in buffers]
        + [pltpu.SemaphoreType.DMA((SEMS,)), pltpu.SemaphoreType.DMA((SEMS,)), pltpu.SemaphoreType.DMA((16,))],
        compiler_params=pltpu.CompilerParams(collective_id=0, has_side_effects=True, vmem_limit_bytes=56 * 2**20),
        name="layer",
    )(*(pltpu.with_memory_space_constraint(a, pltpu.HBM) for a in arrays))
    patch_grad, inner_grad, *others = results
    return (patch_grad.reshape(320, 640), inner_grad.T, *others)


def solution(mesh):
    in_specs = (
        P(("gy", "gz"), "gx"),
        P("gx", ("gy", "gz")),
        P(("gy", "gz"), "gx"),
        P("gx", ("gy", "gz")),
        P("gx", ("gy", "gz")),
        P(("gy", "gz"), "gx"),
        P(("gy", "gz"), "gx"),
    )
    out_specs = (
        P(None, "gx"),
        P("gx", ("gy", "gz")),
        P(("gy", "gz"), "gx"),
        P("gx", ("gy", "gz")),
        P("gx", ("gy", "gz")),
        P(("gy", "gz"), "gx"),
    )
    return jax.shard_map(local, mesh=mesh, in_specs=in_specs, out_specs=out_specs, check_vma=False)
```
